256 devices in a mesh: ch: 4 (over y_lo, core), sp: 64 (over y_hi, z, x).
Axes of the slice: x: 4, y: 4 (y_hi: 2, y_lo: 2; y = y_hi * 2 + y_lo), z: 8, core: 2. Of those that a mesh axis runs over, the one named last changes fastest.
Arguments:
- latents: bfloat16 [256, 64, 90, 128], P('ch', 'sp'), may hold values from -6 to 6
- space_weight: bfloat16 [256, 9, 256], P('ch'), may hold values from -0.125 to 0.125
- space_bias: float32 [256], P('ch'), may hold values from -3 to 3
- time_weight: bfloat16 [3, 256, 256], P(None, 'ch'), may hold values from -0.21875 to 0.21875
- time_bias: float32 [256], P('ch'), may hold values from -3 to 3
Outputs:
- decoded: bfloat16 [256, 64, 90, 128], P('ch', 'sp')
The draws below stay inside these ranges and needn't reach their ends.
All inputs are finite; a program needn't handle non-finite values.
Results may differ from the reference program's by a relative error of at most 0.0046.
Values may be sent and summed in bfloat16 or wider, within the bound.
A program may use at most 128 MiB of HBM per device.

```python
import jax
import jax.numpy as jnp
from jax import lax

C = 256
H = 90
W = 128
FRAMES = 64


def level_of(rng, shape, split, low, largest):
    factor_of, own = 1.0, jax.random.fold_in(rng, 6)
    for axis_at, parts in split:
        steps = jnp.exp(jax.random.uniform(jax.random.fold_in(own, axis_at), (parts,), jnp.float32, low / len(split), largest / len(split)))
        factor_of = factor_of * jnp.repeat(steps, shape[axis_at] // parts).reshape([-1 if axis == axis_at else 1 for axis in range(len(shape))])
    return factor_of


def scatter_about(key, shape, width, bound, pieces=(), kind=jnp.bfloat16):
    loudness = level_of(key, shape, pieces, -0.22, 0.18) if pieces else 1.0
    drawn = jax.random.normal(key, shape, jnp.float32) * width * loudness
    return jnp.minimum(jnp.maximum(drawn, -bound), bound).astype(kind)


def setup_inputs(seed: int = 0) -> dict:
    arg_keys = jax.random.split(jax.random.key(seed), 6)
    latents = scatter_about(arg_keys[0], (C, FRAMES, H, W), 1.0, 6.0, ((0, 4), (1, 64)))
    space_weight = scatter_about(arg_keys[1], (C, 9, C), (9 * C) ** -0.5, 0.125, ((0, 4),))
    space_bias = scatter_about(arg_keys[2], (C,), 0.5, 3.0, ((0, 4),), jnp.float32)
    time_weight = scatter_about(arg_keys[3], (3, C, C), (3 * C) ** -0.5, 0.21875, ((1, 4),))
    time_bias = scatter_about(arg_keys[4], (C,), 0.5, 3.0, ((0, 4),), jnp.float32)
    return {"latents": latents, "space_weight": space_weight, "space_bias": space_bias, "time_weight": time_weight, "time_bias": time_bias}


def reference(latents, space_weight, space_bias, time_weight, time_bias):
    rows = latents.shape[2]
    cols = latents.shape[3]
    frames_first = jnp.moveaxis(latents, 1, 0)
    weight_space = space_weight.astype(jnp.float32)

    def spatial_frame(frame):
        padded = jnp.pad(frame, ((0, 0), (1, 1), (1, 1))).astype(jnp.float32)
        total = jnp.zeros((frame.shape[0], rows, cols), jnp.float32)
        for tap in range(9):
            row_off, col_off = divmod(tap, 3)
            window = padded[:, row_off:row_off + rows, col_off:col_off + cols]
            total = total + jnp.einsum("oi,ihw->ohw", weight_space[:, tap, :], window)
        total = total + space_bias[:, None, None]
        return jax.nn.silu(total).astype(jnp.bfloat16)

    hidden = lax.map(spatial_frame, frames_first)
    count = hidden.shape[0]
    flat = hidden.reshape(count, hidden.shape[1], rows * cols)
    padded_time = jnp.concatenate([jnp.zeros((2,) + flat.shape[1:], jnp.bfloat16), flat], axis=0)
    weight_time = time_weight.astype(jnp.float32)
    inputs_flat = frames_first.reshape(count, frames_first.shape[1], rows * cols)

    def temporal_frame(index):
        window = lax.dynamic_slice_in_dim(padded_time, index, 3, 0).astype(jnp.float32)
        total = jnp.zeros(window.shape[1:], jnp.float32)
        for lag in range(3):
            total = total + jnp.einsum("oi,ip->op", weight_time[lag], window[2 - lag])
        temporal = (total + time_bias[:, None]).astype(jnp.bfloat16)
        current = lax.dynamic_index_in_dim(inputs_flat, index, 0, keepdims=False)
        return (current.astype(jnp.float32) + temporal.astype(jnp.float32)).astype(jnp.bfloat16)

    result = lax.map(temporal_frame, jnp.arange(count, dtype=jnp.int32))
    result = result.reshape(count, result.shape[1], rows, cols)
    return jnp.moveaxis(result, 0, 1)
```

```python
import functools

import jax
import jax.numpy as jnp
from jax import lax
from jax.experimental import pallas as pl
from jax.experimental.pallas import tpu as pltpu
from jax.sharding import PartitionSpec as P

MESH = pl.DeviceIdType.MESH
ROWS, COLS, CH, SHARD = 90, 128, 256, 64
PITCH = 96
NZ = 8
SPACE_K, TIME_K = 9 * CH, 3 * CH
ORDER = ((1, 2), (3, 0), (2, 3), (0, 2), (1, 0), (3, 2), (2, 0), (0, 3), (1, 3), (3, 1), (2, 2), (1, 1), (3, 3), (2, 1), (0, 1))


def chip_start(chip):
    return (45 * chip) // 4


def kernel(
    lat_hbm, weight_hbm, bias_hbm, out_ref,
    lat, flat, sent, taken, left, right, hidden, made, back, weight, bias, own_weight, own_bias,
    load_sem, in_send, in_recv, z_send, z_recv, swap_send, swap_recv, w_send, w_recv, out_send, out_recv,
):
    sp, q = lax.axis_index("sp"), lax.axis_index("ch")
    x = lax.rem(sp, 4)
    row_of_frames = sp // 4
    base = row_of_frames * 4
    z, yh = lax.rem(row_of_frames, NZ), row_of_frames // NZ
    hi, core = q // 2, lax.rem(q, 2)
    me = x * 4 + q
    has_prev = row_of_frames > 0
    has_next = row_of_frames < 2 * NZ - 1
    start = chip_start(2 * x + hi)
    short = lax.rem(2 * x + hi, 4) < 3

    def device(dx, fc):
        nx = lax.rem(x + dx, 4)
        nq = lax.rem(hi + fc // 2, 2) * 2 + lax.rem(core + fc % 2, 2)
        return nx, nq

    def ident(nx, nq):
        return {"sp": base + nx, "ch": nq}

    partner = {"sp": sp, "ch": hi * 2 + 1 - core}
    across = {"sp": (1 - yh) * 4 * NZ + z * 4 + x, "ch": (1 - hi) * 2 + core}

    loads = []
    for part in range(4):
        piece = pl.ds(part * 16, 16)
        copy = pltpu.make_async_copy(lat_hbm.at[piece, 0], lat.at[piece, pl.ds(0, ROWS)], load_sem.at[part])
        copy.start()
        loads.append(copy)
    load_weight = pltpu.make_async_copy(weight_hbm, own_weight, load_sem.at[4])
    load_bias = pltpu.make_async_copy(bias_hbm, own_bias, load_sem.at[5])
    load_weight.start()
    load_bias.start()
    barrier = pltpu.get_barrier_semaphore()
    for dx, fc in ORDER:
        pl.semaphore_signal(barrier, inc=1, device_id=ident(*device(dx, fc)), device_id_type=MESH)
    pl.semaphore_signal(barrier, inc=1, device_id=across, device_id_type=MESH)

    @pl.when(has_prev)
    def _():
        pl.semaphore_signal(barrier, inc=1, device_id={"sp": sp - 4, "ch": q}, device_id_type=MESH)

    sent[0] = jnp.zeros((SHARD, COLS), jnp.bfloat16)
    sent[ROWS + 1] = jnp.zeros((SHARD, COLS), jnp.bfloat16)
    for part in range(4):
        loads[part].wait()

        @pl.loop(part * 16, part * 16 + 16)
        def _(c):
            flat[pl.ds(pl.multiple_of(c * PITCH, PITCH), PITCH), :] = lat[c].astype(jnp.float32)

    @pl.loop(0, ROWS)
    def _(r):
        sent[r + 1] = flat[pl.ds(r, SHARD, stride=PITCH), :].astype(jnp.bfloat16)

    pl.semaphore_wait(barrier, 16 + has_next.astype(jnp.int32))

    load_weight.wait()
    load_bias.wait()
    weight_rows = pl.ds(pl.multiple_of(q * SHARD, SHARD), SHARD)
    weight_copies = []
    for i, there in enumerate((across, partner)):
        for j, (src, dst) in enumerate(((own_weight, weight), (own_bias, bias))):
            copy = pltpu.make_async_remote_copy(
                src_ref=src, dst_ref=dst.at[weight_rows], send_sem=w_send.at[2 * i + j], recv_sem=w_recv.at[2 * i + j],
                device_id=there, device_id_type=MESH,
            )
            copy.start()
            weight_copies.append(copy)
    keep_weight = pltpu.make_async_copy(own_weight, weight.at[weight_rows], load_sem.at[4])
    keep_bias = pltpu.make_async_copy(own_bias, bias.at[weight_rows], load_sem.at[5])
    keep_weight.start()
    keep_bias.start()

    def in_piece(chunk, t_chip, t_core):
        if chunk == 0:
            return chip_start(t_chip) + 10 * t_core, 4 * t_core, 4
        return chip_start(t_chip) + 4 + 3 * t_core, 4 - 3 * t_core, 3

    my_channels = pl.ds(pl.multiple_of(q * SHARD, SHARD), SHARD)
    in_copies = []
    for chunk in range(2):
        for k, (dx, fc) in enumerate(ORDER):
            nx, nq = device(dx, fc)
            src, dst, n = in_piece(chunk, 2 * nx + nq // 2, lax.rem(nq, 2))
            copy = pltpu.make_async_remote_copy(
                src_ref=sent.at[pl.ds(src, n)], dst_ref=taken.at[2 + x, pl.ds(dst, n), my_channels],
                send_sem=in_send.at[chunk, k], recv_sem=in_recv.at[chunk, me],
                device_id=ident(nx, nq), device_id_type=MESH,
            )
            copy.start()
            in_copies.append(copy)
        src, dst, n = in_piece(chunk, 2 * x + hi, core)
        pltpu.make_async_copy(
            sent.at[pl.ds(src, n)], taken.at[2 + x, pl.ds(dst, n), my_channels], in_recv.at[chunk, me]
        ).start()

    def z_copy(chunk, sx, sq):
        _, dst, n = in_piece(chunk, 0, core)
        return pltpu.make_async_remote_copy(
            src_ref=taken.at[2 + sx, pl.ds(dst, n), pl.ds(sq * SHARD, SHARD)],
            dst_ref=taken.at[sx - 2, pl.ds(dst, n), pl.ds(sq * SHARD, SHARD)],
            send_sem=z_send.at[chunk, (sx - 2) * 4 + sq], recv_sem=z_recv.at[chunk, (sx - 2) * 4 + sq],
            device_id={"sp": jnp.minimum(sp + 4, 8 * NZ - 1), "ch": q}, device_id_type=MESH,
        )

    def arrive(chunk):
        _, dst, n = in_piece(chunk, 0, core)
        for sx in (2, 3, 0, 1):
            for sq in range(4):
                got = taken.at[2 + sx, pl.ds(dst, n), pl.ds(sq * SHARD, SHARD)]
                pltpu.make_async_copy(got, got, in_recv.at[chunk, sx * 4 + sq]).wait()
                if sx >= 2:
                    pl.when(has_next)(lambda sx=sx, sq=sq: z_copy(chunk, sx, sq).start())

    def arrive_z(chunk):
        for sx in (2, 3):
            for sq in range(4):
                z_copy(chunk, sx, sq).wait_recv()

    def shift(slot, idx):
        row = taken[slot, idx].astype(jnp.float32)
        lane = lax.broadcasted_iota(jnp.int32, row.shape, 1)
        left[slot, idx] = jnp.where(lane == 0, 0.0, pltpu.roll(row, 1, 1)).astype(jnp.bfloat16)
        right[slot, idx] = jnp.where(lane == COLS - 1, 0.0, pltpu.roll(row, COLS - 1, 1)).astype(jnp.bfloat16)

    def conv(slot, pair):
        taps = []
        for dy in range(3):
            for buf in (left, taken, right):
                taps.append(jnp.concatenate([buf[slot, 2 * pair + dy], buf[slot, 2 * pair + dy + 1]], axis=1))
        rhs = jnp.concatenate(taps, axis=0)
        v = jnp.dot(weight[:, :SPACE_K], rhs, preferred_element_type=jnp.float32) + bias[:, 0:1]
        h = (v / (1.0 + jnp.exp(-v))).astype(jnp.bfloat16)
        hidden[slot, 2 * pair] = h[:, :COLS]
        hidden[slot, 2 * pair + 1] = h[:, COLS:]

    def temporal(frame, pair):
        lags = [
            jnp.concatenate([hidden[frame + 2 - lag, 2 * pair], hidden[frame + 2 - lag, 2 * pair + 1]], axis=1)
            for lag in range(3)
        ]
        rhs = jnp.concatenate(lags, axis=0)
        v = jnp.dot(weight[:, SPACE_K:], rhs, preferred_element_type=jnp.float32) + bias[:, 1:2]
        y = v.astype(jnp.bfloat16)
        made[frame, 2 * pair] = y[:, :COLS]
        made[frame, 2 * pair + 1] = y[:, COLS:]

    first_row = start + 6 * core

    def home_copy(frame, tq, pair, step, n):
        src = made.at[frame, pl.ds(2 * pair, n), pl.ds(pl.multiple_of(tq * SHARD, SHARD), SHARD)]
        dst = back.at[pl.ds(first_row + 2 * pair, n)]
        return src, dst, pltpu.make_async_remote_copy(
            src_ref=src, dst_ref=dst, send_sem=out_send.at[step, frame, tq], recv_sem=out_recv,
            device_id={"sp": base + frame, "ch": tq}, device_id_type=MESH,
        )

    def each_home(frame, pair, step, act_far, act_self):
        lacks = jnp.logical_and(jnp.logical_and(core == 1, short), pair == 2)
        for tq in range(4):
            is_me = jnp.logical_and(frame == x, tq == q)
            for n, fits in ((2, jnp.logical_not(lacks)), (1, lacks)):
                src, dst, far = home_copy(frame, tq, pair, step, n)
                pl.when(jnp.logical_and(fits, jnp.logical_not(is_me)))(functools.partial(act_far, far))
                pl.when(jnp.logical_and(fits, is_me))(functools.partial(act_self, src, dst))

    def go_home(frame, pair, step):
        each_home(
            frame, pair, step, lambda far: far.start(),
            lambda src, dst: pltpu.make_async_copy(src, dst, out_recv).start(),
        )

    def do_pair(pair, step):
        @pl.loop(2, 6)
        def _(slot):
            conv(slot, pair)

        @pl.loop(2, 4)
        def _(frame):
            temporal(frame, pair)
            go_home(frame, pair, step)

    def do_pair_z(pair, step):
        @pl.when(has_prev)
        def _():
            @pl.loop(0, 2)
            def _(slot):
                conv(slot, pair)

        @pl.when(jnp.logical_not(has_prev))
        def _():
            zero = jnp.zeros((CH, COLS), jnp.bfloat16)
            for slot in range(2):
                for k in range(2):
                    hidden[slot, 2 * pair + k] = zero

        @pl.loop(0, 2)
        def _(frame):
            temporal(frame, pair)
            go_home(frame, pair, step)

    def shift_rows(lo, hi_, idx0, n):
        @pl.loop(lo * n, hi_ * n)
        def _(i):
            shift(i // n, idx0 + lax.rem(i, n))

    arrive(0)
    for copy in weight_copies[:2]:
        copy.wait_recv()
    theirs = pl.ds(pl.multiple_of(((1 - hi) * 2 + core) * SHARD, SHARD), SHARD)
    passed = []
    for j, ref in enumerate((weight, bias)):
        copy = pltpu.make_async_remote_copy(
            src_ref=ref.at[theirs], dst_ref=ref.at[theirs], send_sem=w_send.at[4 + j], recv_sem=w_recv.at[4 + j],
            device_id=partner, device_id_type=MESH,
        )
        copy.start()
        passed.append(copy)
    shift_rows(2, 6, 4 * core, 4)
    for copy in weight_copies[2:] + passed:
        copy.wait_recv()
    keep_weight.wait()
    keep_bias.wait()
    do_pair(2 * core, 0)

    @pl.when(has_prev)
    def _():
        arrive_z(0)
        shift_rows(0, 2, 4 * core, 4)

    do_pair_z(2 * core, 0)

    arrive(1)

    def swap(lo, n, k):
        return pltpu.make_async_remote_copy(
            src_ref=taken.at[pl.ds(lo, n), 6 - 5 * core], dst_ref=taken.at[pl.ds(lo, n), 7 * core],
            send_sem=swap_send.at[k], recv_sem=swap_recv.at[k], device_id=partner, device_id_type=MESH,
        )

    swap(2, 4, 0).start()
    shift_rows(2, 6, 4 - 3 * core, 3)
    do_pair(1, 1)
    swap(2, 4, 0).wait_recv()

    @pl.loop(2, 6)
    def _(slot):
        shift(slot, 7 * (1 - core))

    do_pair(2 - 2 * core, 2)

    @pl.when(has_prev)
    def _():
        arrive_z(1)
        swap(0, 2, 1).start()
        shift_rows(0, 2, 4 - 3 * core, 3)

    do_pair_z(1, 1)

    @pl.when(has_prev)
    def _():
        swap(0, 2, 1).wait_recv()

        @pl.loop(0, 2)
        def _(slot):
            shift(slot, 7 * (1 - core))

    do_pair_z(2 - 2 * core, 2)

    pltpu.make_async_copy(back, back, out_recv).wait()

    @pl.loop(0, ROWS)
    def _(r):
        flat[pl.ds(pl.multiple_of(r * SHARD, SHARD), SHARD), :] = back[r].astype(jnp.float32)

    @pl.loop(0, SHARD)
    def _(c):
        temporal_rows = flat[pl.ds(c, ROWS, stride=SHARD), :]
        out_ref[c, 0] = (lat[c, :ROWS].astype(jnp.float32) + temporal_rows).astype(jnp.bfloat16)

    for copy in weight_copies + passed:
        copy.wait_send()
    for copy in in_copies:
        copy.wait_send()

    @pl.when(has_next)
    def _():
        for chunk in range(2):
            for sx in (2, 3):
                for sq in range(4):
                    z_copy(chunk, sx, sq).wait_send()

    swap(2, 4, 0).wait_send()

    @pl.when(has_prev)
    def _():
        swap(0, 2, 1).wait_send()

    for step, pair in ((0, 2 * core), (1, 1), (2, 2 - 2 * core)):
        @pl.loop(0, 4)
        def _(frame):
            each_home(frame, pair, step, lambda far: far.wait_send(), lambda src, dst: None)


def on_device(latents, space_weight, space_bias, time_weight, time_bias):
    weight = jnp.concatenate(
        [space_weight.reshape(SHARD, SPACE_K), time_weight.transpose(1, 0, 2).reshape(SHARD, TIME_K)], axis=1
    )
    bias = jnp.pad(jnp.stack([space_bias, time_bias], axis=1), ((0, 0), (0, COLS - 2)))
    vmem, dma = pltpu.VMEM, pltpu.SemaphoreType.DMA
    bf16, f32 = jnp.bfloat16, jnp.float32
    return pl.pallas_call(
        kernel,
        out_shape=jax.ShapeDtypeStruct(latents.shape, bf16),
        in_specs=[pl.BlockSpec(memory_space=pl.ANY)] * 3,
        out_specs=pl.BlockSpec(memory_space=pltpu.VMEM),
        scratch_shapes=[
            vmem((SHARD, PITCH, COLS), bf16),
            vmem((SHARD * PITCH, COLS), f32),
            vmem((ROWS + 2, SHARD, COLS), bf16),
            vmem((6, 8, CH, COLS), bf16),
            vmem((6, 8, CH, COLS), bf16),
            vmem((6, 8, CH, COLS), bf16),
            vmem((6, 6, CH, COLS), bf16),
            vmem((4, 6, CH, COLS), bf16),
            vmem((ROWS, SHARD, COLS), bf16),
            vmem((CH, SPACE_K + TIME_K), bf16),
            vmem((CH, COLS), f32),
            vmem((SHARD, SPACE_K + TIME_K), bf16),
            vmem((SHARD, COLS), f32),
            dma((6,)),
            dma((2, 15)),
            dma((2, 16)),
            dma((2, 8)),
            dma((2, 8)),
            dma((2,)),
            dma((2,)),
            dma((6,)),
            dma((6,)),
            dma((3, 4, 4)),
            dma,
        ],
        compiler_params=pltpu.CompilerParams(collective_id=0, has_side_effects=True, vmem_limit_bytes=56 << 20),
        cost_estimate=pl.CostEstimate(flops=6_000_000_000, bytes_accessed=6_000_000, transcendentals=1_200_000),
    )(latents, weight, bias)


def solution(mesh):
    return jax.shard_map(
        on_device,
        mesh=mesh,
        in_specs=(
            P("ch", "sp", None, None),
            P("ch", None, None),
            P("ch"),
            P(None, "ch", None),
            P("ch"),
        ),
        out_specs=P("ch", "sp", None, None),
        check_vma=False,
    )
```

```python
import functools

import jax
import jax.numpy as jnp
from jax import lax
from jax.experimental import pallas as pl
from jax.experimental.pallas import tpu as pltpu
from jax.sharding import PartitionSpec as P

MESH = pl.DeviceIdType.MESH
ROWS, COLS, CH, SHARD = 90, 128, 256, 64
NZ = 8
ORDER = ((1, 2), (3, 0), (2, 3), (0, 2), (1, 0), (3, 2), (2, 0), (0, 3), (1, 3), (3, 1), (2, 2), (1, 1), (3, 3), (2, 1), (0, 1))


def chip_start(chip):
    return (45 * chip) // 4


def kernel(
    lat_hbm, space_hbm, time_hbm, space_bias, time_bias, back,
    sent, taken, left, right, hidden, made, space, time, bias, own_space, own_time, own_bias,
    load_sem, in_send, in_recv, z_send, z_recv, swap_send, swap_recv, w_send, w_recv, out_send, out_recv,
):
    sp, q = lax.axis_index("sp"), lax.axis_index("ch")
    x = lax.rem(sp, 4)
    row_of_frames = sp // 4
    base = row_of_frames * 4
    z, yh = lax.rem(row_of_frames, NZ), row_of_frames // NZ
    hi, core = q // 2, lax.rem(q, 2)
    me = x * 4 + q
    has_prev = row_of_frames > 0
    has_next = row_of_frames < 2 * NZ - 1
    slab = 2 * x + lax.rem(hi + yh, 2)
    start = chip_start(slab)
    short = lax.rem(slab, 4) < 3

    def device(dx, fc):
        nx = lax.rem(x + dx, 4)
        nq = lax.rem(hi + fc // 2, 2) * 2 + lax.rem(core + fc % 2, 2)
        return nx, nq

    def ident(nx, nq):
        return {"sp": base + nx, "ch": nq}

    def along(step):
        turns = z == (NZ - 1 if step > 0 else 0)
        return {"sp": lax.rem(sp + 4 * step + 8 * NZ, 8 * NZ), "ch": jnp.where(turns, (1 - hi) * 2 + core, q)}

    partner = {"sp": sp, "ch": hi * 2 + 1 - core}
    across = {"sp": (1 - yh) * 4 * NZ + z * 4 + x, "ch": (1 - hi) * 2 + core}

    loads = [
        pltpu.make_async_copy(src, dst, load_sem.at[i])
        for i, (src, dst) in enumerate((
            (lat_hbm, sent.at[pl.ds(1, ROWS)]), (space_hbm, own_space), (time_hbm, own_time),
        ))
    ]
    for copy in loads:
        copy.start()
    barrier = pltpu.get_barrier_semaphore()
    for dx, fc in ORDER:
        pl.semaphore_signal(barrier, inc=1, device_id=ident(*device(dx, fc)), device_id_type=MESH)
    pl.semaphore_signal(barrier, inc=1, device_id=across, device_id_type=MESH)

    @pl.when(has_prev)
    def _():
        pl.semaphore_signal(barrier, inc=1, device_id=along(-1), device_id_type=MESH)

    sent[0] = jnp.zeros((SHARD, COLS), jnp.bfloat16)
    sent[ROWS + 1] = jnp.zeros((SHARD, COLS), jnp.bfloat16)
    at = lax.broadcasted_iota(jnp.int32, (SHARD, SHARD), 0) == lax.broadcasted_iota(jnp.int32, (SHARD, SHARD), 1)
    for k, ref in enumerate((space_bias, time_bias)):
        column = jnp.sum(jnp.where(at, ref[...], 0.0), axis=1, keepdims=True)
        own_bias[:, k * SHARD:(k + 1) * SHARD] = jnp.broadcast_to(column, (SHARD, SHARD))
    for copy in loads:
        copy.wait()
    pl.semaphore_wait(barrier, 16 + has_next.astype(jnp.int32))

    def block(of):
        return pl.ds(pl.multiple_of(of * SHARD, SHARD), SHARD)

    parts = (
        (own_space, lambda of: space.at[:, block(of)]),
        (own_time, lambda of: time.at[:, block(of)]),
        (own_bias, lambda of: bias.at[block(of)]),
    )
    weight_copies = []
    for i, there in enumerate((across, partner)):
        for j, (src, dst) in enumerate(parts):
            copy = pltpu.make_async_remote_copy(
                src_ref=src, dst_ref=dst(q), send_sem=w_send.at[3 * i + j], recv_sem=w_recv.at[3 * i + j],
                device_id=there, device_id_type=MESH,
            )
            copy.start()
            weight_copies.append(copy)
    keeps = [pltpu.make_async_copy(src, dst(q), load_sem.at[j]) for j, (src, dst) in enumerate(parts)]
    for copy in keeps:
        copy.start()

    def in_piece(chunk, t_chip, t_core):
        if chunk == 0:
            return chip_start(t_chip) + 10 * t_core, 4 * t_core, 4
        return chip_start(t_chip) + 4 + 3 * t_core, 4 - 3 * t_core, 3

    my_channels = block(q)
    in_copies = []
    for chunk in range(2):
        for k, (dx, fc) in enumerate(ORDER):
            nx, nq = device(dx, fc)
            src, dst, n = in_piece(chunk, 2 * nx + lax.rem(nq // 2 + yh, 2), lax.rem(nq, 2))
            copy = pltpu.make_async_remote_copy(
                src_ref=sent.at[pl.ds(src, n)], dst_ref=taken.at[2 + x, pl.ds(dst, n), my_channels],
                send_sem=in_send.at[chunk, k], recv_sem=in_recv.at[chunk, me],
                device_id=ident(nx, nq), device_id_type=MESH,
            )
            copy.start()
            in_copies.append(copy)
        src, dst, n = in_piece(chunk, slab, core)
        pltpu.make_async_copy(
            sent.at[pl.ds(src, n)], taken.at[2 + x, pl.ds(dst, n), my_channels], in_recv.at[chunk, me]
        ).start()

    def z_copy(chunk, sx, sq):
        _, dst, n = in_piece(chunk, 0, core)
        return pltpu.make_async_remote_copy(
            src_ref=taken.at[2 + sx, pl.ds(dst, n), pl.ds(sq * SHARD, SHARD)],
            dst_ref=taken.at[sx - 2, pl.ds(dst, n), pl.ds(sq * SHARD, SHARD)],
            send_sem=z_send.at[chunk, (sx - 2) * 4 + sq], recv_sem=z_recv.at[chunk, (sx - 2) * 4 + sq],
            device_id=along(1), device_id_type=MESH,
        )

    def arrive(chunk):
        _, dst, n = in_piece(chunk, 0, core)
        for sx in (2, 3, 0, 1):
            for sq in range(4):
                got = taken.at[2 + sx, pl.ds(dst, n), pl.ds(sq * SHARD, SHARD)]
                pltpu.make_async_copy(got, got, in_recv.at[chunk, sx * 4 + sq]).wait()
                if sx >= 2:
                    pl.when(has_next)(lambda sx=sx, sq=sq: z_copy(chunk, sx, sq).start())

    def arrive_z(chunk):
        for sx in (2, 3):
            for sq in range(4):
                z_copy(chunk, sx, sq).wait_recv()

    def shift(slot, idx):
        row = taken[slot, idx].astype(jnp.float32)
        lane = lax.broadcasted_iota(jnp.int32, row.shape, 1)
        left[slot, idx] = jnp.where(lane == 0, 0.0, pltpu.roll(row, 1, 1)).astype(jnp.bfloat16)
        right[slot, idx] = jnp.where(lane == COLS - 1, 0.0, pltpu.roll(row, COLS - 1, 1)).astype(jnp.bfloat16)

    def conv(slot, pair):
        taps = []
        for dy in range(3):
            for buf in (left, taken, right):
                taps.append(jnp.concatenate([buf[slot, 2 * pair + dy], buf[slot, 2 * pair + dy + 1]], axis=1))
        lhs = jnp.concatenate([space[tap] for tap in range(9)], axis=1)
        v = jnp.dot(lhs, jnp.concatenate(taps, axis=0), preferred_element_type=jnp.float32) + bias[:, 0:1]
        h = (v / (1.0 + jnp.exp(-v))).astype(jnp.bfloat16)
        hidden[slot, 2 * pair] = h[:, :COLS]
        hidden[slot, 2 * pair + 1] = h[:, COLS:]

    def temporal(frame, pair):
        lags = [
            jnp.concatenate([hidden[frame + 2 - lag, 2 * pair], hidden[frame + 2 - lag, 2 * pair + 1]], axis=1)
            for lag in range(3)
        ]
        lhs = jnp.concatenate([time[lag] for lag in range(3)], axis=1)
        v = jnp.dot(lhs, jnp.concatenate(lags, axis=0), preferred_element_type=jnp.float32) + bias[:, SHARD:SHARD + 1]
        y = v.astype(jnp.bfloat16)
        made[frame, 2 * pair] = y[:, :COLS]
        made[frame, 2 * pair + 1] = y[:, COLS:]

    first_row = start + 6 * core

    def home_copy(frame, tq, pair, step, n):
        src = made.at[frame, pl.ds(2 * pair, n), pl.ds(pl.multiple_of(tq * SHARD, SHARD), SHARD)]
        dst = back.at[pl.ds(first_row + 2 * pair, n)]
        return src, dst, pltpu.make_async_remote_copy(
            src_ref=src, dst_ref=dst, send_sem=out_send.at[step, frame, tq], recv_sem=out_recv,
            device_id={"sp": base + frame, "ch": tq}, device_id_type=MESH,
        )

    def each_home(frame, pair, step, act_far, act_self):
        lacks = jnp.logical_and(jnp.logical_and(core == 1, short), pair == 2)
        for tq in range(4):
            is_me = jnp.logical_and(frame == x, tq == q)
            for n, fits in ((2, jnp.logical_not(lacks)), (1, lacks)):
                src, dst, far = home_copy(frame, tq, pair, step, n)
                pl.when(jnp.logical_and(fits, jnp.logical_not(is_me)))(functools.partial(act_far, far))
                pl.when(jnp.logical_and(fits, is_me))(functools.partial(act_self, src, dst))

    def go_home(frame, pair, step):
        each_home(
            frame, pair, step, lambda far: far.start(),
            lambda src, dst: pltpu.make_async_copy(src, dst, out_recv).start(),
        )

    def do_pair(pair, step):
        @pl.loop(2, 6)
        def _(slot):
            conv(slot, pair)

        @pl.loop(2, 4)
        def _(frame):
            temporal(frame, pair)
            go_home(frame, pair, step)

    def do_pair_z(pair, step):
        @pl.when(has_prev)
        def _():
            @pl.loop(0, 2)
            def _(slot):
                conv(slot, pair)

        @pl.when(jnp.logical_not(has_prev))
        def _():
            zero = jnp.zeros((CH, COLS), jnp.bfloat16)
            for slot in range(2):
                for k in range(2):
                    hidden[slot, 2 * pair + k] = zero

        @pl.loop(0, 2)
        def _(frame):
            temporal(frame, pair)
            go_home(frame, pair, step)

    def shift_rows(lo, hi_, idx0, n):
        @pl.loop(lo * n, hi_ * n)
        def _(i):
            shift(i // n, idx0 + lax.rem(i, n))

    arrive(0)
    for copy in weight_copies[:3]:
        copy.wait_recv()
    theirs = (1 - hi) * 2 + core
    passed = []
    for j, (_, dst) in enumerate(parts):
        copy = pltpu.make_async_remote_copy(
            src_ref=dst(theirs), dst_ref=dst(theirs), send_sem=w_send.at[6 + j], recv_sem=w_recv.at[6 + j],
            device_id=partner, device_id_type=MESH,
        )
        copy.start()
        passed.append(copy)
    shift_rows(2, 6, 4 * core, 4)
    for copy in weight_copies[3:] + passed:
        copy.wait_recv()
    for copy in keeps:
        copy.wait()
    do_pair(2 * core, 0)

    @pl.when(has_prev)
    def _():
        arrive_z(0)
        shift_rows(0, 2, 4 * core, 4)

    do_pair_z(2 * core, 0)

    arrive(1)

    def swap(lo, n, k):
        return pltpu.make_async_remote_copy(
            src_ref=taken.at[pl.ds(lo, n), 6 - 5 * core], dst_ref=taken.at[pl.ds(lo, n), 7 * core],
            send_sem=swap_send.at[k], recv_sem=swap_recv.at[k], device_id=partner, device_id_type=MESH,
        )

    swap(2, 4, 0).start()
    shift_rows(2, 6, 4 - 3 * core, 3)
    do_pair(1, 1)
    swap(2, 4, 0).wait_recv()

    @pl.loop(2, 6)
    def _(slot):
        shift(slot, 7 * (1 - core))

    do_pair(2 - 2 * core, 2)

    @pl.when(has_prev)
    def _():
        arrive_z(1)
        swap(0, 2, 1).start()
        shift_rows(0, 2, 4 - 3 * core, 3)

    do_pair_z(1, 1)

    @pl.when(has_prev)
    def _():
        swap(0, 2, 1).wait_recv()

        @pl.loop(0, 2)
        def _(slot):
            shift(slot, 7 * (1 - core))

    do_pair_z(2 - 2 * core, 2)

    pltpu.make_async_copy(back, back, out_recv).wait()

    for copy in weight_copies + passed:
        copy.wait_send()
    for copy in in_copies:
        copy.wait_send()

    @pl.when(has_next)
    def _():
        for chunk in range(2):
            for sx in (2, 3):
                for sq in range(4):
                    z_copy(chunk, sx, sq).wait_send()

    swap(2, 4, 0).wait_send()

    @pl.when(has_prev)
    def _():
        swap(0, 2, 1).wait_send()

    for step, pair in ((0, 2 * core), (1, 1), (2, 2 - 2 * core)):
        @pl.loop(0, 4)
        def _(frame):
            each_home(frame, pair, step, lambda far: far.wait_send(), lambda src, dst: None)


def on_device(latents, space_weight, space_bias, time_weight, time_bias):
    rows_first = latents[:, 0].transpose(1, 0, 2)
    vmem, dma = pltpu.VMEM, pltpu.SemaphoreType.DMA
    bf16, f32 = jnp.bfloat16, jnp.float32
    temporal = pl.pallas_call(
        kernel,
        out_shape=jax.ShapeDtypeStruct(rows_first.shape, bf16),
        in_specs=[pl.BlockSpec(memory_space=pltpu.HBM)] * 3 + [pl.BlockSpec(memory_space=pltpu.VMEM)] * 2,
        out_specs=pl.BlockSpec(memory_space=pl.ANY),
        scratch_shapes=[
            vmem((ROWS + 2, SHARD, COLS), bf16),
            vmem((6, 8, CH, COLS), bf16),
            vmem((6, 8, CH, COLS), bf16),
            vmem((6, 8, CH, COLS), bf16),
            vmem((6, 6, CH, COLS), bf16),
            vmem((4, 6, CH, COLS), bf16),
            vmem((9, CH, CH), bf16),
            vmem((3, CH, CH), bf16),
            vmem((CH, COLS), f32),
            vmem((9, SHARD, CH), bf16),
            vmem((3, SHARD, CH), bf16),
            vmem((SHARD, COLS), f32),
            dma((4,)),
            dma((2, 15)),
            dma((2, 16)),
            dma((2, 8)),
            dma((2, 8)),
            dma((2,)),
            dma((2,)),
            dma((9,)),
            dma((9,)),
            dma((3, 4, 4)),
            dma,
        ],
        compiler_params=pltpu.CompilerParams(collective_id=0, has_side_effects=True, vmem_limit_bytes=62 << 20),
        cost_estimate=pl.CostEstimate(flops=6_000_000_000, bytes_accessed=6_000_000, transcendentals=1_200_000),
    )(rows_first, space_weight.transpose(1, 0, 2), time_weight, space_bias[None], time_bias[None])
    total = rows_first.astype(f32) + temporal.astype(f32)
    return total.astype(bf16).transpose(1, 0, 2)[:, None]


def solution(mesh):
    return jax.shard_map(
        on_device,
        mesh=mesh,
        in_specs=(
            P("ch", "sp", None, None),
            P("ch", None, None),
            P("ch"),
            P(None, "ch", None),
            P("ch"),
        ),
        out_specs=P("ch", "sp", None, None),
        check_vma=False,
    )
```

```python
import functools

import jax
import jax.numpy as jnp
from jax import lax
from jax.experimental import pallas as pl
from jax.experimental.pallas import tpu as pltpu
from jax.sharding import PartitionSpec as P

MESH = pl.DeviceIdType.MESH
ROWS, COLS, CH, SHARD = 90, 128, 256, 64
NZ = 8
ORDER = ((1, 2), (3, 0), (2, 3), (0, 2), (1, 0), (3, 2), (2, 0), (0, 3), (1, 3), (3, 1), (2, 2), (1, 1), (3, 3), (2, 1), (0, 1))


def chip_start(chip):
    return (45 * chip) // 4


def chunk_start(chip, core):
    return chip_start(chip) + 6 * core


def kernel(
    lat_hbm, space_hbm, time_hbm, space_bias, time_bias, back,
    sent, taken, hidden, made, space, time, bias, own_space, own_time, own_bias,
    load_sem, in_send, in_recv, z_send, z_recv, swap_send, swap_recv, w_send, w_recv, out_send, out_recv,
):
    sp, q = lax.axis_index("sp"), lax.axis_index("ch")
    x = lax.rem(sp, 4)
    row_of_frames = sp // 4
    base = row_of_frames * 4
    z, yh = lax.rem(row_of_frames, NZ), row_of_frames // NZ
    hi, core = q // 2, lax.rem(q, 2)
    me = x * 4 + q
    has_prev = row_of_frames > 0
    has_next = row_of_frames < 2 * NZ - 1
    slab = 2 * x + lax.rem(hi + yh, 2)
    start = chip_start(slab)
    short = lax.rem(slab, 4) < 3

    def device(dx, fc):
        nx = lax.rem(x + dx, 4)
        nq = lax.rem(hi + fc // 2, 2) * 2 + lax.rem(core + fc % 2, 2)
        return nx, nq

    def ident(nx, nq):
        return {"sp": base + nx, "ch": nq}

    def along(step):
        turns = z == (NZ - 1 if step > 0 else 0)
        return {"sp": lax.rem(sp + 4 * step + 8 * NZ, 8 * NZ), "ch": jnp.where(turns, (1 - hi) * 2 + core, q)}

    partner = {"sp": sp, "ch": hi * 2 + 1 - core}
    across = {"sp": (1 - yh) * 4 * NZ + z * 4 + x, "ch": (1 - hi) * 2 + core}

    loads = [
        pltpu.make_async_copy(src, dst, load_sem.at[i])
        for i, (src, dst) in enumerate((
            (lat_hbm, sent.at[pl.ds(1, ROWS)]), (space_hbm, own_space), (time_hbm, own_time),
        ))
    ]
    for copy in loads:
        copy.start()
    barrier = pltpu.get_barrier_semaphore()
    for dx, fc in ORDER:
        pl.semaphore_signal(barrier, inc=1, device_id=ident(*device(dx, fc)), device_id_type=MESH)
    pl.semaphore_signal(barrier, inc=1, device_id=across, device_id_type=MESH)

    @pl.when(has_prev)
    def _():
        pl.semaphore_signal(barrier, inc=1, device_id=along(-1), device_id_type=MESH)

    sent[0] = jnp.zeros((SHARD, COLS), jnp.bfloat16)
    sent[ROWS + 1] = jnp.zeros((SHARD, COLS), jnp.bfloat16)
    at = lax.broadcasted_iota(jnp.int32, (SHARD, SHARD), 0) == lax.broadcasted_iota(jnp.int32, (SHARD, SHARD), 1)
    for k, ref in enumerate((space_bias, time_bias)):
        column = jnp.sum(jnp.where(at, ref[...], 0.0), axis=1, keepdims=True)
        own_bias[:, k * SHARD:(k + 1) * SHARD] = jnp.broadcast_to(column, (SHARD, SHARD))
    for copy in loads:
        copy.wait()
    pl.semaphore_wait(barrier, 16 + has_next.astype(jnp.int32))

    def block(of):
        return pl.ds(pl.multiple_of(of * SHARD, SHARD), SHARD)

    parts = (
        (own_space, lambda of: space.at[:, block(of)]),
        (own_time, lambda of: time.at[:, block(of)]),
        (own_bias, lambda of: bias.at[block(of)]),
    )
    weight_copies = []
    for i, there in enumerate((across, partner)):
        for j, (src, dst) in enumerate(parts):
            copy = pltpu.make_async_remote_copy(
                src_ref=src, dst_ref=dst(q), send_sem=w_send.at[3 * i + j], recv_sem=w_recv.at[3 * i + j],
                device_id=there, device_id_type=MESH,
            )
            copy.start()
            weight_copies.append(copy)
    keeps = [pltpu.make_async_copy(src, dst(q), load_sem.at[j]) for j, (src, dst) in enumerate(parts)]
    for copy in keeps:
        copy.start()

    chunk_rows = (4, 2, 1)

    def chunk_at(chunk, of_core):
        return (4 * of_core, 4 - 2 * of_core, 6 - 5 * of_core)[chunk]

    my_channels = block(q)
    def in_source(chunk, t_slab, t_core):
        return sent.at[pl.ds(chunk_start(t_slab, t_core) + chunk_at(chunk, t_core), chunk_rows[chunk])]

    def in_target(chunk, slot, of_core, channels):
        return taken.at[slot, pl.ds(chunk_at(chunk, of_core), chunk_rows[chunk]), channels]

    in_copies = []
    for chunk in range(3):
        pltpu.make_async_copy(
            in_source(chunk, slab, core), in_target(chunk, 2 + x, core, my_channels), in_recv.at[chunk, me]
        ).start()
        for k, (dx, fc) in enumerate(ORDER):
            nx, nq = device(dx, fc)
            t_core = lax.rem(nq, 2)
            copy = pltpu.make_async_remote_copy(
                src_ref=in_source(chunk, 2 * nx + lax.rem(nq // 2 + yh, 2), t_core),
                dst_ref=in_target(chunk, 2 + x, t_core, my_channels),
                send_sem=in_send.at[chunk, k], recv_sem=in_recv.at[chunk, me],
                device_id=ident(nx, nq), device_id_type=MESH,
            )
            copy.start()
            in_copies.append(copy)

    def z_copy(chunk, frame, sq):
        return pltpu.make_async_remote_copy(
            src_ref=in_target(chunk, 4 + frame, core, block(sq)), dst_ref=in_target(chunk, frame, core, block(sq)),
            send_sem=z_send.at[chunk, frame * 4 + sq], recv_sem=z_recv.at[chunk, frame * 4 + sq],
            device_id=along(1), device_id_type=MESH,
        )

    def arrive(chunk):
        for dx, fc in ((0, 0),) + ORDER:
            sx, sq = lax.rem(x + 4 - dx, 4), device(dx, fc)[1]
            got = in_target(chunk, 2 + sx, core, block(sq))
            pltpu.make_async_copy(got, got, in_recv.at[chunk, sx * 4 + sq]).wait()

            @pl.when(jnp.logical_and(has_next, sx >= 2))
            def _():
                z_copy(chunk, sx - 2, sq).start()

    def arrive_z(chunk):
        for frame in range(2):
            for sq in range(4):
                z_copy(chunk, frame, sq).wait_recv()

    lane = lax.broadcasted_iota(jnp.int32, (CH, COLS), 1)
    first_lane, last_lane = lane == 0, lane == COLS - 1

    def conv(slot, pair):
        rows = []
        for k in range(4):
            row = taken[slot, 2 * pair + k]
            zero = jnp.zeros_like(row)
            rows.append((
                jnp.where(first_lane, zero, pltpu.roll(row, 1, 1)), row,
                jnp.where(last_lane, zero, pltpu.roll(row, COLS - 1, 1)),
            ))
        taps = [
            jnp.concatenate([rows[dy][dx], rows[dy + 1][dx]], axis=1) for dy in range(3) for dx in range(3)
        ]
        lhs = jnp.concatenate([space[tap] for tap in range(9)], axis=1)
        v = jnp.dot(lhs, jnp.concatenate(taps, axis=0), preferred_element_type=jnp.float32) + bias[:, 0:1]
        half = 0.5 * v
        h = (half + half * jnp.tanh(half)).astype(jnp.bfloat16)
        hidden[slot, 2 * pair] = h[:, :COLS]
        hidden[slot, 2 * pair + 1] = h[:, COLS:]

    def temporal(frame, pair):
        lags = [
            jnp.concatenate([hidden[frame + 2 - lag, 2 * pair], hidden[frame + 2 - lag, 2 * pair + 1]], axis=1)
            for lag in range(3)
        ]
        lhs = jnp.concatenate([time[lag] for lag in range(3)], axis=1)
        v = jnp.dot(lhs, jnp.concatenate(lags, axis=0), preferred_element_type=jnp.float32) + bias[:, SHARD:SHARD + 1]
        y = v.astype(jnp.bfloat16)
        made[frame, 2 * pair] = y[:, :COLS]
        made[frame, 2 * pair + 1] = y[:, COLS:]

    first_row = start + 6 * core

    def home_copy(frame, tq, pair, step, n):
        src = made.at[frame, pl.ds(2 * pair, n), pl.ds(pl.multiple_of(tq * SHARD, SHARD), SHARD)]
        dst = back.at[pl.ds(first_row + 2 * pair, n)]
        return src, dst, pltpu.make_async_remote_copy(
            src_ref=src, dst_ref=dst, send_sem=out_send.at[step, frame, tq], recv_sem=out_recv,
            device_id={"sp": base + frame, "ch": tq}, device_id_type=MESH,
        )

    def each_home(frame, pair, step, act_far, act_self):
        lacks = jnp.logical_and(jnp.logical_and(core == 1, short), pair == 2)
        for tq in range(4):
            is_me = jnp.logical_and(frame == x, tq == q)
            for n, fits in ((2, jnp.logical_not(lacks)), (1, lacks)):
                src, dst, far = home_copy(frame, tq, pair, step, n)
                pl.when(jnp.logical_and(fits, jnp.logical_not(is_me)))(functools.partial(act_far, far))
                pl.when(jnp.logical_and(fits, is_me))(functools.partial(act_self, src, dst))

    def go_home(frame, pair, step):
        each_home(
            frame, pair, step, lambda far: far.start(),
            lambda src, dst: pltpu.make_async_copy(src, dst, out_recv).start(),
        )

    def swap(lo, n, k):
        return pltpu.make_async_remote_copy(
            src_ref=taken.at[pl.ds(lo, n), 6 - 5 * core], dst_ref=taken.at[pl.ds(lo, n), 7 * core],
            send_sem=swap_send.at[k], recv_sem=swap_recv.at[k], device_id=partner, device_id_type=MESH,
        )

    arrive(0)
    for copy in weight_copies[:3]:
        copy.wait_recv()
    theirs = (1 - hi) * 2 + core
    passed = []
    for j, (_, dst) in enumerate(parts):
        copy = pltpu.make_async_remote_copy(
            src_ref=dst(theirs), dst_ref=dst(theirs), send_sem=w_send.at[6 + j], recv_sem=w_recv.at[6 + j],
            device_id=partner, device_id_type=MESH,
        )
        copy.start()
        passed.append(copy)
    for copy in weight_copies[3:] + passed:
        copy.wait_recv()
    for copy in keeps:
        copy.wait()

    @pl.loop(0, 3)
    def _(step):
        pair = 2 * core + step * (1 - 2 * core)

        @pl.when(step == 2)
        def _():
            swap(2, 4, 0).wait_recv()

        for slot in range(2, 6):
            conv(slot, pair)
        for frame in (2, 3):
            temporal(frame, pair)
        for frame in (2, 3):
            go_home(frame, pair, step)

        for chunk in (1, 2):
            @pl.when(step == chunk - 1)
            def _():
                arrive(chunk)
                if chunk == 2:
                    swap(2, 4, 0).start()

        @pl.when(has_prev)
        def _():
            for chunk in range(3):
                @pl.when(step == chunk)
                def _():
                    arrive_z(chunk)
                    if chunk == 2:
                        swap(0, 2, 1).start()
                        swap(0, 2, 1).wait_recv()

            for slot in range(2):
                conv(slot, pair)

        @pl.when(jnp.logical_not(has_prev))
        def _():
            zero = jnp.zeros((CH, COLS), jnp.bfloat16)
            for slot in range(2):
                for k in range(2):
                    hidden[slot, 2 * pair + k] = zero

        for frame in range(2):
            temporal(frame, pair)
        for frame in range(2):
            go_home(frame, pair, step)

    pltpu.make_async_copy(back, back, out_recv).wait()

    for copy in weight_copies + passed:
        copy.wait_send()
    for copy in in_copies:
        copy.wait_send()

    @pl.when(has_next)
    def _():
        for chunk in range(3):
            for frame in range(2):
                for sq in range(4):
                    z_copy(chunk, frame, sq).wait_send()

    swap(2, 4, 0).wait_send()

    @pl.when(has_prev)
    def _():
        swap(0, 2, 1).wait_send()

    @pl.loop(0, 3)
    def _(step):
        for frame in range(4):
            each_home(
                frame, 2 * core + step * (1 - 2 * core), step, lambda far: far.wait_send(), lambda src, dst: None
            )


def on_device(latents, space_weight, space_bias, time_weight, time_bias):
    rows_first = latents[:, 0].transpose(1, 0, 2)
    vmem, dma = pltpu.VMEM, pltpu.SemaphoreType.DMA
    bf16, f32 = jnp.bfloat16, jnp.float32
    temporal = pl.pallas_call(
        kernel,
        out_shape=jax.ShapeDtypeStruct(rows_first.shape, bf16),
        in_specs=[pl.BlockSpec(memory_space=pltpu.HBM)] * 3 + [pl.BlockSpec(memory_space=pltpu.VMEM)] * 2,
        out_specs=pl.BlockSpec(memory_space=pl.ANY),
        scratch_shapes=[
            vmem((ROWS + 2, SHARD, COLS), bf16),
            vmem((6, 8, CH, COLS), bf16),
            vmem((6, 6, CH, COLS), bf16),
            vmem((4, 6, CH, COLS), bf16),
            vmem((9, CH, CH), bf16),
            vmem((3, CH, CH), bf16),
            vmem((CH, COLS), f32),
            vmem((9, SHARD, CH), bf16),
            vmem((3, SHARD, CH), bf16),
            vmem((SHARD, COLS), f32),
            dma((4,)),
            dma((3, 15)),
            dma((3, 16)),
            dma((3, 8)),
            dma((3, 8)),
            dma((2,)),
            dma((2,)),
            dma((9,)),
            dma((9,)),
            dma((3, 4, 4)),
            dma,
        ],
        compiler_params=pltpu.CompilerParams(collective_id=0, has_side_effects=True, vmem_limit_bytes=62 << 20),
        cost_estimate=pl.CostEstimate(flops=6_000_000_000, bytes_accessed=6_000_000, transcendentals=1_200_000),
    )(rows_first, space_weight.transpose(1, 0, 2), time_weight, space_bias[None], time_bias[None])
    total = rows_first.astype(f32) + temporal.astype(f32)
    return total.astype(bf16).transpose(1, 0, 2)[:, None]


def solution(mesh):
    return jax.shard_map(
        on_device,
        mesh=mesh,
        in_specs=(
            P("ch", "sp", None, None),
            P("ch", None, None),
            P("ch"),
            P(None, "ch", None),
            P("ch"),
        ),
        out_specs=P("ch", "sp", None, None),
        check_vma=False,
    )
```

```python
import functools

import jax
import jax.numpy as jnp
from jax import lax
from jax.experimental import pallas as pl
from jax.experimental.pallas import tpu as pltpu
from jax.sharding import PartitionSpec as P

MESH = pl.DeviceIdType.MESH
ROWS, COLS, CH, SHARD = 90, 128, 256, 64
NZ = 8
ORDER = ((1, 2), (3, 0), (2, 3), (0, 2), (1, 0), (3, 2), (2, 0), (0, 3), (1, 3), (3, 1), (2, 2), (1, 1), (3, 3), (2, 1), (0, 1))


CHUNKS = ((2, 0, 3, 1), (2, 0, 5, 3), (2, 1, 1, 5), (1, 2, 0, 7))
EDGE = len(CHUNKS) - 1


def chip_start(chip):
    return (45 * chip) // 4


def chunk_start(chip, core):
    return chip_start(chip) + 6 * core


def kernel(
    lat_hbm, space_hbm, time_hbm, space_bias, time_bias, back,
    taken, hidden, made, space, time, bias, own_bias, raw_bias,
    keep_sem, in_send, in_recv, z_send, z_recv, swap_send, swap_recv, w_send, w_recv, out_send, out_recv,
):
    sp, q = lax.axis_index("sp"), lax.axis_index("ch")
    x = lax.rem(sp, 4)
    row_of_frames = sp // 4
    base = row_of_frames * 4
    z, yh = lax.rem(row_of_frames, NZ), row_of_frames // NZ
    hi, core = q // 2, lax.rem(q, 2)
    me = x * 4 + q
    has_prev = row_of_frames > 0
    has_next = row_of_frames < 2 * NZ - 1
    slab = 2 * x + lax.rem(hi + yh, 2)
    start = chip_start(slab)
    short = lax.rem(slab, 4) < 3

    def device(dx, fc):
        nx = lax.rem(x + dx, 4)
        nq = lax.rem(hi + fc // 2, 2) * 2 + lax.rem(core + fc % 2, 2)
        return nx, nq

    def ident(nx, nq):
        return {"sp": base + nx, "ch": nq}

    def along(step):
        turns = z == (NZ - 1 if step > 0 else 0)
        return {"sp": lax.rem(sp + 4 * step + 8 * NZ, 8 * NZ), "ch": jnp.where(turns, (1 - hi) * 2 + core, q)}

    crosses, relays, skips = row_of_frames == NZ, row_of_frames == 2 * NZ - 1, row_of_frames == 0
    ring_end = {"sp": 4 * (2 * NZ - 1) + x, "ch": q}
    ring_start = {"sp": 4 * NZ + x, "ch": q}
    partner = {"sp": sp, "ch": hi * 2 + 1 - core}
    across = {"sp": (1 - yh) * 4 * NZ + z * 4 + x, "ch": (1 - hi) * 2 + core}

    bias_loads = [
        pltpu.make_async_copy(src, raw_bias.at[k], keep_sem.at[4 + k]) for k, src in enumerate((space_bias, time_bias))
    ]
    for copy in bias_loads:
        copy.start()

    barrier = pltpu.get_barrier_semaphore()
    for dx, fc in ORDER:
        pl.semaphore_signal(barrier, inc=1, device_id=ident(*device(dx, fc)), device_id_type=MESH)
    pl.semaphore_signal(barrier, inc=1, device_id=across, device_id_type=MESH)

    @pl.when(has_prev)
    def _():
        pl.semaphore_signal(barrier, inc=1, device_id=along(-1), device_id_type=MESH)

    def has_edge(of_slab, of_core):
        return jnp.where(of_core == 0, of_slab != 0, of_slab == 3)

    edge = has_edge(slab, core)

    @pl.when(jnp.logical_not(edge))
    def _():
        for slot in range(6):
            taken[slot, 7 * core] = jnp.zeros((CH, COLS), jnp.bfloat16)

    @pl.when(crosses)
    def _():
        pl.semaphore_signal(barrier, inc=1, device_id=ring_end, device_id_type=MESH)

    pl.semaphore_wait(barrier, 17)

    def block(of):
        return pl.ds(pl.multiple_of(of * SHARD, SHARD), SHARD)

    parts = (
        (space_hbm.at[pl.ds(0, 6)], lambda of: space.at[pl.ds(0, 6), block(of)]),
        (space_hbm.at[pl.ds(6, 3)], lambda of: space.at[pl.ds(6, 3), block(of)]),
        (time_hbm, lambda of: time.at[:, block(of)]),
        (own_bias, lambda of: bias.at[block(of)]),
    )
    def weight_copy(j, of, there, k):
        src, dst = parts[j]
        return pltpu.make_async_remote_copy(
            src_ref=src if k < 8 else dst(of), dst_ref=dst(of), send_sem=w_send.at[k], recv_sem=w_recv.at[k % 12],
            device_id=there, device_id_type=MESH,
        )

    keeps = [pltpu.make_async_copy(src, dst(q), keep_sem.at[j]) for j, (src, dst) in enumerate(parts)]
    theirs = (1 - hi) * 2 + core

    def send_weight(j):
        if j == 0:
            pl.when(jnp.logical_not(skips))(weight_copy(j, q, across, j).start)
        else:
            weight_copy(j, q, across, j).start()
        weight_copy(j, q, partner, 4 + j).start()
        keeps[j].start()

    my_channels = block(q)

    def chunk_at(chunk, of_core):
        _, _, low, high = CHUNKS[chunk]
        return low + (high - low) * of_core

    def in_source(chunk, t_slab, t_core):
        first = chip_start(t_slab) - 1 + 6 * t_core + chunk_at(chunk, t_core)
        return lat_hbm.at[pl.ds(first, CHUNKS[chunk][0])]

    def in_target(chunk, slot, of_core, channels):
        return taken.at[slot, pl.ds(chunk_at(chunk, of_core), CHUNKS[chunk][0]), channels]

    in_copies = []
    for chunk in range(len(CHUNKS)):
        if chunk == 1:
            for j in range(3):
                send_weight(j)
        pl.when(jnp.logical_or(chunk < EDGE, edge))(
            pltpu.make_async_copy(
                in_source(chunk, slab, core), in_target(chunk, 2 + x, core, my_channels), in_recv.at[chunk, me]
            ).start
        )
        for k, (dx, fc) in enumerate(ORDER):
            nx, nq = device(dx, fc)
            t_slab, t_core = 2 * nx + lax.rem(nq // 2 + yh, 2), lax.rem(nq, 2)
            copy = pltpu.make_async_remote_copy(
                src_ref=in_source(chunk, t_slab, t_core),
                dst_ref=in_target(chunk, 2 + x, t_core, my_channels),
                send_sem=in_send.at[chunk, k], recv_sem=in_recv.at[chunk, me],
                device_id=ident(nx, nq), device_id_type=MESH,
            )
            sends = jnp.logical_or(chunk < EDGE, has_edge(t_slab, t_core))
            pl.when(sends)(copy.start)
            in_copies.append((sends, copy))

    for copy in bias_loads:
        copy.wait()
    raw_bias_rows = [raw_bias[0], raw_bias[1]]
    at = lax.broadcasted_iota(jnp.int32, (SHARD, SHARD), 0) == lax.broadcasted_iota(jnp.int32, (SHARD, SHARD), 1)
    for k, ref in enumerate(raw_bias_rows):
        column = jnp.sum(jnp.where(at, ref, 0.0), axis=1, keepdims=True)
        own_bias[:, k * SHARD:(k + 1) * SHARD] = jnp.broadcast_to(column, (SHARD, SHARD))
    send_weight(3)

    def z_copy(chunk, frame, sq):
        return pltpu.make_async_remote_copy(
            src_ref=in_target(chunk, 4 + frame, core, block(sq)), dst_ref=in_target(chunk, frame, core, block(sq)),
            send_sem=z_send.at[chunk, frame * 4 + sq], recv_sem=z_recv.at[chunk, frame * 4 + sq],
            device_id=along(1), device_id_type=MESH,
        )

    def step_chunks(step):
        return [chunk for chunk in range(len(CHUNKS)) if CHUNKS[chunk][1] == step]

    def arrive(step):
        for chunk in step_chunks(step):
            pl.when(jnp.logical_or(chunk < EDGE, edge))(functools.partial(arrive_chunk, chunk))

    def arrive_chunk(chunk):
        for dx, fc in ((0, 0),) + ORDER:
            sx, sq = lax.rem(x + 4 - dx, 4), device(dx, fc)[1]
            got = in_target(chunk, 2 + sx, core, block(sq))
            pltpu.make_async_copy(got, got, in_recv.at[chunk, sx * 4 + sq]).wait()

            @pl.when(jnp.logical_and(has_next, sx >= 2))
            def _():
                z_copy(chunk, sx - 2, sq).start()

    def arrive_z(step):
        for chunk in step_chunks(step):
            @pl.when(jnp.logical_or(chunk < EDGE, edge))
            def _():
                for frame in range(2):
                    for sq in range(4):
                        z_copy(chunk, frame, sq).wait_recv()

    lane = lax.broadcasted_iota(jnp.int32, (CH, COLS), 1)
    first_lane, last_lane = lane == 0, lane == COLS - 1

    def conv(slot, pair):
        rows = []
        for k in range(4):
            row = taken[slot, 2 * pair + k]
            zero = jnp.zeros_like(row)
            rows.append((
                jnp.where(first_lane, zero, pltpu.roll(row, 1, 1)), row,
                jnp.where(last_lane, zero, pltpu.roll(row, COLS - 1, 1)),
            ))
        taps = [
            jnp.concatenate([rows[dy][dx], rows[dy + 1][dx]], axis=1) for dy in range(3) for dx in range(3)
        ]
        lhs = jnp.concatenate([space[tap] for tap in range(9)], axis=1)
        v = jnp.dot(lhs, jnp.concatenate(taps, axis=0), preferred_element_type=jnp.float32) + bias[:, 0:1]
        half = 0.5 * v
        h = (half + half * jnp.tanh(half)).astype(jnp.bfloat16)
        hidden[slot, 2 * pair] = h[:, :COLS]
        hidden[slot, 2 * pair + 1] = h[:, COLS:]

    def temporal(frame, pair):
        lags = [
            jnp.concatenate([hidden[frame + 2 - lag, 2 * pair], hidden[frame + 2 - lag, 2 * pair + 1]], axis=1)
            for lag in range(3)
        ]
        lhs = jnp.concatenate([time[lag] for lag in range(3)], axis=1)
        v = jnp.dot(lhs, jnp.concatenate(lags, axis=0), preferred_element_type=jnp.float32) + bias[:, SHARD:SHARD + 1]
        y = v.astype(jnp.bfloat16).astype(jnp.float32)
        for k in range(2):
            own = taken[frame + 2, 2 * pair + 1 + k].astype(jnp.float32)
            made[frame, 2 * pair + k] = (own + y[:, k * COLS:(k + 1) * COLS]).astype(jnp.bfloat16)

    first_row = start + 6 * core

    def home_copy(frame, tq, pair, step, n):
        src = made.at[frame, pl.ds(2 * pair, n), pl.ds(pl.multiple_of(tq * SHARD, SHARD), SHARD)]
        dst = back.at[pl.ds(first_row + 2 * pair, n)]
        return src, dst, pltpu.make_async_remote_copy(
            src_ref=src, dst_ref=dst, send_sem=out_send.at[step, frame, tq], recv_sem=out_recv,
            device_id={"sp": base + frame, "ch": tq}, device_id_type=MESH,
        )

    def each_home(frame, pair, step, act_far, act_self):
        lacks = jnp.logical_and(jnp.logical_and(core == 1, short), pair == 2)
        for tq in range(4):
            is_me = jnp.logical_and(frame == x, tq == q)
            for n, fits in ((2, jnp.logical_not(lacks)), (1, lacks)):
                src, dst, far = home_copy(frame, tq, pair, step, n)
                pl.when(jnp.logical_and(fits, jnp.logical_not(is_me)))(functools.partial(act_far, far))
                pl.when(jnp.logical_and(fits, is_me))(functools.partial(act_self, src, dst))

    def go_home(frame, pair, step):
        each_home(
            frame, pair, step, lambda far: far.start(),
            lambda src, dst: pltpu.make_async_copy(src, dst, out_recv).start(),
        )

    def swap(lo, n, k):
        return pltpu.make_async_remote_copy(
            src_ref=taken.at[pl.ds(lo, n), 6 - 5 * core], dst_ref=taken.at[pl.ds(lo, n), 7 * core],
            send_sem=swap_send.at[k], recv_sem=swap_recv.at[k], device_id=partner, device_id_type=MESH,
        )

    @pl.when(relays)
    def _():
        weight_copy(0, q, across, 0).wait_recv()
        weight_copy(0, theirs, ring_start, 12).start()

    arrive(0)
    swap(2, 4, 0).start()
    pl.when(jnp.logical_not(relays))(weight_copy(0, q, across, 0).wait_recv)
    for j in range(4):
        if j > 0:
            weight_copy(j, q, across, j).wait_recv()
        weight_copy(j, theirs, partner, 8 + j).start()
    for j in range(4):
        weight_copy(j, q, partner, 4 + j).wait_recv()
        weight_copy(j, theirs, partner, 8 + j).wait_recv()
        keeps[j].wait()
    swap(2, 4, 0).wait_recv()

    def pair_of(step):
        return 2 * (1 - core) + step * (2 * core - 1)

    @pl.loop(0, 3)
    def _(step):
        pair = pair_of(step)

        for slot in range(2, 6):
            conv(slot, pair)
        for frame in (2, 3):
            temporal(frame, pair)
        for frame in (2, 3):
            go_home(frame, pair, step)

        for later in (1, 2):
            pl.when(step == later - 1)(functools.partial(arrive, later))

        @pl.when(has_prev)
        def _():
            for now in range(3):
                @pl.when(step == now)
                def _():
                    arrive_z(now)
                    if now == 0:
                        swap(0, 2, 1).start()
                        swap(0, 2, 1).wait_recv()

            for slot in range(2):
                conv(slot, pair)

        @pl.when(jnp.logical_not(has_prev))
        def _():
            zero = jnp.zeros((CH, COLS), jnp.bfloat16)
            for slot in range(2):
                for k in range(2):
                    hidden[slot, 2 * pair + k] = zero

        for frame in range(2):
            temporal(frame, pair)
        for frame in range(2):
            go_home(frame, pair, step)

    pl.when(jnp.logical_not(skips))(weight_copy(0, q, across, 0).wait_send)
    pl.when(relays)(weight_copy(0, theirs, ring_start, 12).wait_send)
    for j in range(4):
        if j > 0:
            weight_copy(j, q, across, j).wait_send()
        weight_copy(j, q, partner, 4 + j).wait_send()
        weight_copy(j, theirs, partner, 8 + j).wait_send()
    for sends, copy in in_copies:
        pl.when(sends)(copy.wait_send)

    @pl.when(has_next)
    def _():
        for chunk in range(len(CHUNKS)):
            for frame in range(2):
                for sq in range(4):
                    pl.when(jnp.logical_or(chunk < EDGE, edge))(z_copy(chunk, frame, sq).wait_send)

    swap(2, 4, 0).wait_send()

    @pl.when(has_prev)
    def _():
        swap(0, 2, 1).wait_send()

    @pl.loop(0, 3)
    def _(step):
        for frame in range(4):
            each_home(
                frame, pair_of(step), step, lambda far: far.wait_send(), lambda src, dst: None
            )

    pltpu.make_async_copy(back, back, out_recv).wait()


def on_device(latents, space_weight, space_bias, time_weight, time_bias):
    rows_first = latents[:, 0].transpose(1, 0, 2)
    vmem, dma = pltpu.VMEM, pltpu.SemaphoreType.DMA
    bf16, f32 = jnp.bfloat16, jnp.float32
    decoded = pl.pallas_call(
        kernel,
        out_shape=pltpu.VMEM(rows_first.shape, bf16),
        in_specs=[pl.BlockSpec(memory_space=pl.ANY)] * 5,
        out_specs=pl.BlockSpec(memory_space=pl.ANY),
        scratch_shapes=[
            vmem((6, 8, CH, COLS), bf16),
            vmem((6, 6, CH, COLS), bf16),
            vmem((4, 6, CH, COLS), bf16),
            vmem((9, CH, CH), bf16),
            vmem((3, CH, CH), bf16),
            vmem((CH, COLS), f32),
            vmem((SHARD, COLS), f32),
            vmem((2, 1, SHARD), f32),
            dma((6,)),
            dma((len(CHUNKS), 15)),
            dma((len(CHUNKS), 16)),
            dma((len(CHUNKS), 8)),
            dma((len(CHUNKS), 8)),
            dma((2,)),
            dma((2,)),
            dma((13,)),
            dma((12,)),
            dma((3, 4, 4)),
            dma,
        ],
        compiler_params=pltpu.CompilerParams(collective_id=0, has_side_effects=True, vmem_limit_bytes=62 << 20),
        cost_estimate=pl.CostEstimate(flops=6_000_000_000, bytes_accessed=6_000_000, transcendentals=1_200_000),
    )(rows_first, space_weight.transpose(1, 0, 2), time_weight, space_bias[None], time_bias[None])
    return decoded.transpose(1, 0, 2)[:, None]


def solution(mesh):
    return jax.shard_map(
        on_device,
        mesh=mesh,
        in_specs=(
            P("ch", "sp", None, None),
            P("ch", None, None),
            P("ch"),
            P(None, "ch", None),
            P("ch"),
        ),
        out_specs=P("ch", "sp", None, None),
        check_vma=False,
    )
```

```python
import functools

import jax
import jax.numpy as jnp
from jax import lax
from jax.experimental import pallas as pl
from jax.experimental.pallas import tpu as pltpu
from jax.sharding import PartitionSpec as P

MESH = pl.DeviceIdType.MESH
ROWS, COLS, CH, SHARD = 90, 128, 256, 64
NZ = 8
ORDER = ((1, 2), (3, 0), (2, 3), (0, 2), (1, 0), (3, 2), (2, 0), (0, 3), (1, 3), (3, 1), (2, 2), (1, 1), (3, 3), (2, 1), (0, 1))


CHUNKS = ((2, 0, 3, 1), (2, 0, 5, 3), (2, 1, 1, 5), (1, 2, 0, 7))
EDGE = len(CHUNKS) - 1


def chip_start(chip):
    return (45 * chip) // 4


def chunk_start(chip, core):
    return chip_start(chip) + 6 * core


def kernel(
    lat_hbm, space_hbm, time_hbm, space_bias, time_bias, back,
    taken, hidden, made, space, time, bias, own_bias, raw_bias,
    keep_sem, in_send, in_recv, z_send, z_recv, swap_send, swap_recv, w_send, w_recv, out_send, out_recv,
):
    sp, q = lax.axis_index("sp"), lax.axis_index("ch")
    x = lax.rem(sp, 4)
    row_of_frames = sp // 4
    base = row_of_frames * 4
    z, yh = lax.rem(row_of_frames, NZ), row_of_frames // NZ
    hi, core = q // 2, lax.rem(q, 2)
    me = x * 4 + q
    has_prev = row_of_frames > 0
    has_next = row_of_frames < 2 * NZ - 1
    slab = 2 * x + lax.rem(hi + yh, 2)
    start = chip_start(slab)
    short = lax.rem(slab, 4) < 3

    def device(dx, fc):
        nx = lax.rem(x + dx, 4)
        nq = lax.rem(hi + fc // 2, 2) * 2 + lax.rem(core + fc % 2, 2)
        return nx, nq

    def ident(nx, nq):
        return {"sp": base + nx, "ch": nq}

    def along(step):
        turns = z == (NZ - 1 if step > 0 else 0)
        return {"sp": lax.rem(sp + 4 * step + 8 * NZ, 8 * NZ), "ch": jnp.where(turns, (1 - hi) * 2 + core, q)}

    crosses, relays, skips = row_of_frames == NZ, row_of_frames == 2 * NZ - 1, row_of_frames == 0
    ring_end = {"sp": 4 * (2 * NZ - 1) + x, "ch": q}
    ring_start = {"sp": 4 * NZ + x, "ch": q}
    partner = {"sp": sp, "ch": hi * 2 + 1 - core}
    across = {"sp": (1 - yh) * 4 * NZ + z * 4 + x, "ch": (1 - hi) * 2 + core}

    bias_loads = [
        pltpu.make_async_copy(src, raw_bias.at[k], keep_sem.at[4 + k]) for k, src in enumerate((space_bias, time_bias))
    ]
    for copy in bias_loads:
        copy.start()

    barrier = pltpu.get_barrier_semaphore()
    for dx, fc in ORDER:
        pl.semaphore_signal(barrier, inc=1, device_id=ident(*device(dx, fc)), device_id_type=MESH)
    pl.semaphore_signal(barrier, inc=1, device_id=across, device_id_type=MESH)

    @pl.when(has_prev)
    def _():
        pl.semaphore_signal(barrier, inc=1, device_id=along(-1), device_id_type=MESH)

    def has_edge(of_slab, of_core):
        return jnp.where(of_core == 0, of_slab != 0, of_slab == 3)

    edge = has_edge(slab, core)

    @pl.when(jnp.logical_not(edge))
    def _():
        for slot in range(6):
            taken[slot, 7 * core] = jnp.zeros((CH, COLS), jnp.bfloat16)

    @pl.when(crosses)
    def _():
        pl.semaphore_signal(barrier, inc=1, device_id=ring_end, device_id_type=MESH)

    pl.semaphore_wait(barrier, 17)

    def block(of):
        return pl.ds(pl.multiple_of(of * SHARD, SHARD), SHARD)

    parts = (
        (space_hbm.at[pl.ds(0, 6)], lambda of: space.at[pl.ds(0, 6), block(of)]),
        (space_hbm.at[pl.ds(6, 3)], lambda of: space.at[pl.ds(6, 3), block(of)]),
        (time_hbm, lambda of: time.at[:, block(of)]),
        (own_bias, lambda of: bias.at[block(of)]),
    )
    def weight_copy(j, of, there, k):
        src, dst = parts[j]
        return pltpu.make_async_remote_copy(
            src_ref=src if k < 8 else dst(of), dst_ref=dst(of), send_sem=w_send.at[k], recv_sem=w_recv.at[k % 12],
            device_id=there, device_id_type=MESH,
        )

    keeps = [pltpu.make_async_copy(src, dst(q), keep_sem.at[j]) for j, (src, dst) in enumerate(parts)]
    theirs = (1 - hi) * 2 + core

    def send_weight(j):
        if j == 0:
            pl.when(jnp.logical_not(skips))(weight_copy(j, q, across, j).start)
        else:
            weight_copy(j, q, across, j).start()
        weight_copy(j, q, partner, 4 + j).start()
        keeps[j].start()

    my_channels = block(q)

    def chunk_at(chunk, of_core):
        _, _, low, high = CHUNKS[chunk]
        return low + (high - low) * of_core

    def in_source(chunk, t_slab, t_core):
        first = chip_start(t_slab) - 1 + 6 * t_core + chunk_at(chunk, t_core)
        return lat_hbm.at[pl.ds(first, CHUNKS[chunk][0])]

    def in_target(chunk, slot, of_core, channels):
        return taken.at[slot, pl.ds(chunk_at(chunk, of_core), CHUNKS[chunk][0]), channels]

    in_copies = []
    for chunk in range(len(CHUNKS)):
        if chunk == 0:
            for j in range(3):
                send_weight(j)
        pl.when(jnp.logical_or(chunk < EDGE, edge))(
            pltpu.make_async_copy(
                in_source(chunk, slab, core), in_target(chunk, 2 + x, core, my_channels), in_recv.at[chunk, me]
            ).start
        )
        for k, (dx, fc) in enumerate(ORDER):
            nx, nq = device(dx, fc)
            t_slab, t_core = 2 * nx + lax.rem(nq // 2 + yh, 2), lax.rem(nq, 2)
            copy = pltpu.make_async_remote_copy(
                src_ref=in_source(chunk, t_slab, t_core),
                dst_ref=in_target(chunk, 2 + x, t_core, my_channels),
                send_sem=in_send.at[chunk, k], recv_sem=in_recv.at[chunk, me],
                device_id=ident(nx, nq), device_id_type=MESH,
            )
            sends = jnp.logical_or(chunk < EDGE, has_edge(t_slab, t_core))
            pl.when(sends)(copy.start)
            in_copies.append((sends, copy))

    for copy in bias_loads:
        copy.wait()
    raw_bias_rows = [raw_bias[0], raw_bias[1]]
    at = lax.broadcasted_iota(jnp.int32, (SHARD, SHARD), 0) == lax.broadcasted_iota(jnp.int32, (SHARD, SHARD), 1)
    for k, ref in enumerate(raw_bias_rows):
        column = jnp.sum(jnp.where(at, ref, 0.0), axis=1, keepdims=True)
        own_bias[:, k * SHARD:(k + 1) * SHARD] = jnp.broadcast_to(column, (SHARD, SHARD))
    send_weight(3)

    def z_copy(chunk, frame, sq):
        return pltpu.make_async_remote_copy(
            src_ref=in_target(chunk, 4 + frame, core, block(sq)), dst_ref=in_target(chunk, frame, core, block(sq)),
            send_sem=z_send.at[chunk, frame * 4 + sq], recv_sem=z_recv.at[chunk, frame * 4 + sq],
            device_id=along(1), device_id_type=MESH,
        )

    def step_chunks(step):
        return [chunk for chunk in range(len(CHUNKS)) if CHUNKS[chunk][1] == step]

    def arrive(step):
        for chunk in step_chunks(step):
            pl.when(jnp.logical_or(chunk < EDGE, edge))(functools.partial(arrive_chunk, chunk))

    def arrive_chunk(chunk):
        for dx, fc in ((0, 0),) + ORDER:
            sx, sq = lax.rem(x + 4 - dx, 4), device(dx, fc)[1]
            got = in_target(chunk, 2 + sx, core, block(sq))
            pltpu.make_async_copy(got, got, in_recv.at[chunk, sx * 4 + sq]).wait()

            @pl.when(jnp.logical_and(has_next, sx >= 2))
            def _():
                z_copy(chunk, sx - 2, sq).start()

    def arrive_z(step):
        for chunk in step_chunks(step):
            @pl.when(jnp.logical_or(chunk < EDGE, edge))
            def _():
                for frame in range(2):
                    for sq in range(4):
                        z_copy(chunk, frame, sq).wait_recv()

    lane = lax.broadcasted_iota(jnp.int32, (CH, COLS), 1)
    first_lane, last_lane = lane == 0, lane == COLS - 1

    def conv(slot, pair):
        rows = []
        for k in range(4):
            row = taken[slot, 2 * pair + k]
            zero = jnp.zeros_like(row)
            rows.append((
                jnp.where(first_lane, zero, pltpu.roll(row, 1, 1)), row,
                jnp.where(last_lane, zero, pltpu.roll(row, COLS - 1, 1)),
            ))
        taps = [
            jnp.concatenate([rows[dy][dx], rows[dy + 1][dx]], axis=1) for dy in range(3) for dx in range(3)
        ]
        lhs = jnp.concatenate([space[tap] for tap in range(9)], axis=1)
        v = jnp.dot(lhs, jnp.concatenate(taps, axis=0), preferred_element_type=jnp.float32) + bias[:, 0:1]
        half = 0.5 * v
        h = (half + half * jnp.tanh(half)).astype(jnp.bfloat16)
        hidden[slot, 2 * pair] = h[:, :COLS]
        hidden[slot, 2 * pair + 1] = h[:, COLS:]

    def temporal(frame, pair):
        lags = [
            jnp.concatenate([hidden[frame + 2 - lag, 2 * pair], hidden[frame + 2 - lag, 2 * pair + 1]], axis=1)
            for lag in range(3)
        ]
        lhs = jnp.concatenate([time[lag] for lag in range(3)], axis=1)
        v = jnp.dot(lhs, jnp.concatenate(lags, axis=0), preferred_element_type=jnp.float32) + bias[:, SHARD:SHARD + 1]
        y = v.astype(jnp.bfloat16).astype(jnp.float32)
        for k in range(2):
            own = taken[frame + 2, 2 * pair + 1 + k].astype(jnp.float32)
            made[frame, 2 * pair + k] = (own + y[:, k * COLS:(k + 1) * COLS]).astype(jnp.bfloat16)

    first_row = start + 6 * core

    def home_copy(frame, tq, pair, step, n):
        src = made.at[frame, pl.ds(2 * pair, n), pl.ds(pl.multiple_of(tq * SHARD, SHARD), SHARD)]
        dst = back.at[pl.ds(first_row + 2 * pair, n)]
        return src, dst, pltpu.make_async_remote_copy(
            src_ref=src, dst_ref=dst, send_sem=out_send.at[step, frame, tq], recv_sem=out_recv,
            device_id={"sp": base + frame, "ch": tq}, device_id_type=MESH,
        )

    def each_home(frame, pair, step, act_far, act_self):
        lacks = jnp.logical_and(jnp.logical_and(core == 1, short), pair == 2)
        for tq in range(4):
            is_me = jnp.logical_and(frame == x, tq == q)
            for n, fits in ((2, jnp.logical_not(lacks)), (1, lacks)):
                src, dst, far = home_copy(frame, tq, pair, step, n)
                pl.when(jnp.logical_and(fits, jnp.logical_not(is_me)))(functools.partial(act_far, far))
                pl.when(jnp.logical_and(fits, is_me))(functools.partial(act_self, src, dst))

    def go_home(frame, pair, step):
        each_home(
            frame, pair, step, lambda far: far.start(),
            lambda src, dst: pltpu.make_async_copy(src, dst, out_recv).start(),
        )

    def swap(lo, n, k):
        return pltpu.make_async_remote_copy(
            src_ref=taken.at[pl.ds(lo, n), 6 - 5 * core], dst_ref=taken.at[pl.ds(lo, n), 7 * core],
            send_sem=swap_send.at[k], recv_sem=swap_recv.at[k], device_id=partner, device_id_type=MESH,
        )

    @pl.when(relays)
    def _():
        weight_copy(0, q, across, 0).wait_recv()
        weight_copy(0, theirs, ring_start, 12).start()

    arrive(0)
    swap(2, 4, 0).start()
    pl.when(jnp.logical_not(relays))(weight_copy(0, q, across, 0).wait_recv)
    for j in range(4):
        if j > 0:
            weight_copy(j, q, across, j).wait_recv()
        weight_copy(j, theirs, partner, 8 + j).start()
    for j in range(4):
        weight_copy(j, q, partner, 4 + j).wait_recv()
        weight_copy(j, theirs, partner, 8 + j).wait_recv()
        keeps[j].wait()
    swap(2, 4, 0).wait_recv()

    def pair_of(step):
        return 2 * (1 - core) + step * (2 * core - 1)

    @pl.loop(0, 3)
    def _(step):
        pair = pair_of(step)

        for slot in range(2, 6):
            conv(slot, pair)
        for frame in (2, 3):
            temporal(frame, pair)
        @pl.when(step < 2)
        def _():
            for frame in (2, 3):
                go_home(frame, pair, step)

        for later in (1, 2):
            pl.when(step == later - 1)(functools.partial(arrive, later))

        @pl.when(has_prev)
        def _():
            for now in range(3):
                @pl.when(step == now)
                def _():
                    arrive_z(now)
                    if now == 0:
                        swap(0, 2, 1).start()
                        swap(0, 2, 1).wait_recv()

            for slot in range(2):
                conv(slot, pair)

        @pl.when(jnp.logical_not(has_prev))
        def _():
            zero = jnp.zeros((CH, COLS), jnp.bfloat16)
            for slot in range(2):
                for k in range(2):
                    hidden[slot, 2 * pair + k] = zero

        for frame in range(2):
            temporal(frame, pair)
        @pl.when(step < 2)
        def _():
            for frame in range(2):
                go_home(frame, pair, step)

        @pl.when(step == 2)
        def _():
            for ahead in (2, 1, 3, 0):
                go_home(lax.rem(x + ahead, 4), pair, step)

    pl.when(jnp.logical_not(skips))(weight_copy(0, q, across, 0).wait_send)
    pl.when(relays)(weight_copy(0, theirs, ring_start, 12).wait_send)
    for j in range(4):
        if j > 0:
            weight_copy(j, q, across, j).wait_send()
        weight_copy(j, q, partner, 4 + j).wait_send()
        weight_copy(j, theirs, partner, 8 + j).wait_send()
    for sends, copy in in_copies:
        pl.when(sends)(copy.wait_send)

    @pl.when(has_next)
    def _():
        for chunk in range(len(CHUNKS)):
            for frame in range(2):
                for sq in range(4):
                    pl.when(jnp.logical_or(chunk < EDGE, edge))(z_copy(chunk, frame, sq).wait_send)

    swap(2, 4, 0).wait_send()

    @pl.when(has_prev)
    def _():
        swap(0, 2, 1).wait_send()

    @pl.loop(0, 3)
    def _(step):
        for frame in range(4):
            each_home(
                frame, pair_of(step), step, lambda far: far.wait_send(), lambda src, dst: None
            )

    pltpu.make_async_copy(back, back, out_recv).wait()


def on_device(latents, space_weight, space_bias, time_weight, time_bias):
    rows_first = latents[:, 0].transpose(1, 0, 2)
    vmem, dma = pltpu.VMEM, pltpu.SemaphoreType.DMA
    bf16, f32 = jnp.bfloat16, jnp.float32
    decoded = pl.pallas_call(
        kernel,
        out_shape=pltpu.VMEM(rows_first.shape, bf16),
        in_specs=[pl.BlockSpec(memory_space=pl.ANY)] * 5,
        out_specs=pl.BlockSpec(memory_space=pl.ANY),
        scratch_shapes=[
            vmem((6, 8, CH, COLS), bf16),
            vmem((6, 6, CH, COLS), bf16),
            vmem((4, 6, CH, COLS), bf16),
            vmem((9, CH, CH), bf16),
            vmem((3, CH, CH), bf16),
            vmem((CH, COLS), f32),
            vmem((SHARD, COLS), f32),
            vmem((2, 1, SHARD), f32),
            dma((6,)),
            dma((len(CHUNKS), 15)),
            dma((len(CHUNKS), 16)),
            dma((len(CHUNKS), 8)),
            dma((len(CHUNKS), 8)),
            dma((2,)),
            dma((2,)),
            dma((13,)),
            dma((12,)),
            dma((3, 4, 4)),
            dma,
        ],
        compiler_params=pltpu.CompilerParams(collective_id=0, has_side_effects=True, vmem_limit_bytes=62 << 20),
        cost_estimate=pl.CostEstimate(flops=6_000_000_000, bytes_accessed=6_000_000, transcendentals=1_200_000),
    )(rows_first, space_weight.transpose(1, 0, 2), time_weight, space_bias[None], time_bias[None])
    return decoded.transpose(1, 0, 2)[:, None]


def solution(mesh):
    return jax.shard_map(
        on_device,
        mesh=mesh,
        in_specs=(
            P("ch", "sp", None, None),
            P("ch", None, None),
            P("ch"),
            P(None, "ch", None),
            P("ch"),
        ),
        out_specs=P("ch", "sp", None, None),
        check_vma=False,
    )
```

```python
import functools

import jax
import jax.numpy as jnp
from jax import lax
from jax.experimental import pallas as pl
from jax.experimental.pallas import tpu as pltpu
from jax.sharding import PartitionSpec as P

MESH = pl.DeviceIdType.MESH
ROWS, COLS, CH, SHARD = 90, 128, 256, 64
NZ = 8
ORDER = ((1, 2), (3, 0), (2, 3), (0, 2), (1, 0), (3, 2), (2, 0), (0, 3), (1, 3), (3, 1), (2, 2), (1, 1), (3, 3), (2, 1), (0, 1))


CHUNKS = ((4, 0, 3, 1), (2, 1, 1, 5), (1, 2, 0, 7))
EDGE = len(CHUNKS) - 1


def chip_start(chip):
    return (45 * chip) // 4


def chunk_start(chip, core):
    return chip_start(chip) + 6 * core


def kernel(
    lat_hbm, space_hbm, time_hbm, space_bias, time_bias, back,
    taken, hidden, made, space, time, bias, own_bias, raw_bias,
    keep_sem, in_send, in_recv, z_send, z_recv, swap_send, swap_recv, w_send, w_recv, out_send, out_recv,
):
    sp, q = lax.axis_index("sp"), lax.axis_index("ch")
    x = lax.rem(sp, 4)
    row_of_frames = sp // 4
    base = row_of_frames * 4
    z, yh = lax.rem(row_of_frames, NZ), row_of_frames // NZ
    hi, core = q // 2, lax.rem(q, 2)
    me = x * 4 + q
    has_prev = row_of_frames > 0
    has_next = row_of_frames < 2 * NZ - 1
    slab = 2 * x + lax.rem(hi + yh, 2)
    start = chip_start(slab)
    short = lax.rem(slab, 4) < 3

    def device(dx, fc):
        nx = lax.rem(x + dx, 4)
        nq = lax.rem(hi + fc // 2, 2) * 2 + lax.rem(core + fc % 2, 2)
        return nx, nq

    def ident(nx, nq):
        return {"sp": base + nx, "ch": nq}

    def along(step):
        turns = z == (NZ - 1 if step > 0 else 0)
        return {"sp": lax.rem(sp + 4 * step + 8 * NZ, 8 * NZ), "ch": jnp.where(turns, (1 - hi) * 2 + core, q)}

    crosses, relays, skips = row_of_frames == NZ, row_of_frames == 2 * NZ - 1, row_of_frames == 0
    ring_end = {"sp": 4 * (2 * NZ - 1) + x, "ch": q}
    ring_start = {"sp": 4 * NZ + x, "ch": q}
    partner = {"sp": sp, "ch": hi * 2 + 1 - core}
    across = {"sp": (1 - yh) * 4 * NZ + z * 4 + x, "ch": (1 - hi) * 2 + core}

    bias_loads = [
        pltpu.make_async_copy(src, raw_bias.at[k], keep_sem.at[4 + k]) for k, src in enumerate((space_bias, time_bias))
    ]
    for copy in bias_loads:
        copy.start()

    barrier = pltpu.get_barrier_semaphore()
    for dx, fc in ORDER:
        pl.semaphore_signal(barrier, inc=1, device_id=ident(*device(dx, fc)), device_id_type=MESH)
    pl.semaphore_signal(barrier, inc=1, device_id=across, device_id_type=MESH)

    @pl.when(has_prev)
    def _():
        pl.semaphore_signal(barrier, inc=1, device_id=along(-1), device_id_type=MESH)

    def has_edge(of_slab, of_core):
        return jnp.where(of_core == 0, of_slab != 0, of_slab == 3)

    edge = has_edge(slab, core)

    @pl.when(jnp.logical_not(edge))
    def _():
        for slot in range(6):
            taken[slot, 7 * core] = jnp.zeros((CH, COLS), jnp.bfloat16)

    @pl.when(crosses)
    def _():
        pl.semaphore_signal(barrier, inc=1, device_id=ring_end, device_id_type=MESH)

    pl.semaphore_wait(barrier, 17)

    def block(of):
        return pl.ds(pl.multiple_of(of * SHARD, SHARD), SHARD)

    parts = (
        (space_hbm.at[pl.ds(0, 6)], lambda of: space.at[pl.ds(0, 6), block(of)]),
        (space_hbm.at[pl.ds(6, 3)], lambda of: space.at[pl.ds(6, 3), block(of)]),
        (time_hbm, lambda of: time.at[:, block(of)]),
        (own_bias, lambda of: bias.at[block(of)]),
    )
    def weight_copy(j, of, there, k):
        src, dst = parts[j]
        return pltpu.make_async_remote_copy(
            src_ref=src if k < 8 else dst(of), dst_ref=dst(of), send_sem=w_send.at[k], recv_sem=w_recv.at[k % 12],
            device_id=there, device_id_type=MESH,
        )

    keeps = [pltpu.make_async_copy(src, dst(q), keep_sem.at[j]) for j, (src, dst) in enumerate(parts)]
    theirs = (1 - hi) * 2 + core

    def send_weight(j):
        if j == 0:
            pl.when(jnp.logical_not(skips))(weight_copy(j, q, across, j).start)
        else:
            weight_copy(j, q, across, j).start()
        weight_copy(j, q, partner, 4 + j).start()
        keeps[j].start()

    my_channels = block(q)

    def chunk_at(chunk, of_core):
        _, _, low, high = CHUNKS[chunk]
        return low + (high - low) * of_core

    def in_source(chunk, t_slab, t_core):
        first = chip_start(t_slab) - 1 + 6 * t_core + chunk_at(chunk, t_core)
        return lat_hbm.at[pl.ds(first, CHUNKS[chunk][0])]

    def in_target(chunk, slot, of_core, channels):
        return taken.at[slot, pl.ds(chunk_at(chunk, of_core), CHUNKS[chunk][0]), channels]

    in_copies = []
    for chunk in range(len(CHUNKS)):
        if chunk == 0:
            for j in range(3):
                send_weight(j)
        pl.when(jnp.logical_or(chunk < EDGE, edge))(
            pltpu.make_async_copy(
                in_source(chunk, slab, core), in_target(chunk, 2 + x, core, my_channels), in_recv.at[chunk, me]
            ).start
        )
        for k, (dx, fc) in enumerate(ORDER):
            nx, nq = device(dx, fc)
            t_slab, t_core = 2 * nx + lax.rem(nq // 2 + yh, 2), lax.rem(nq, 2)
            copy = pltpu.make_async_remote_copy(
                src_ref=in_source(chunk, t_slab, t_core),
                dst_ref=in_target(chunk, 2 + x, t_core, my_channels),
                send_sem=in_send.at[chunk, k], recv_sem=in_recv.at[chunk, me],
                device_id=ident(nx, nq), device_id_type=MESH,
            )
            sends = jnp.logical_or(chunk < EDGE, has_edge(t_slab, t_core))
            pl.when(sends)(copy.start)
            in_copies.append((sends, copy))

    for copy in bias_loads:
        copy.wait()
    raw_bias_rows = [raw_bias[0], raw_bias[1]]
    at = lax.broadcasted_iota(jnp.int32, (SHARD, SHARD), 0) == lax.broadcasted_iota(jnp.int32, (SHARD, SHARD), 1)
    for k, ref in enumerate(raw_bias_rows):
        column = jnp.sum(jnp.where(at, ref, 0.0), axis=1, keepdims=True)
        own_bias[:, k * SHARD:(k + 1) * SHARD] = jnp.broadcast_to(column, (SHARD, SHARD))
    send_weight(3)

    def z_copy(chunk, frame, sq):
        return pltpu.make_async_remote_copy(
            src_ref=in_target(chunk, 4 + frame, core, block(sq)), dst_ref=in_target(chunk, frame, core, block(sq)),
            send_sem=z_send.at[chunk, frame * 4 + sq], recv_sem=z_recv.at[chunk, frame * 4 + sq],
            device_id=along(1), device_id_type=MESH,
        )

    def step_chunks(step):
        return [chunk for chunk in range(len(CHUNKS)) if CHUNKS[chunk][1] == step]

    def arrive(step):
        for chunk in step_chunks(step):
            pl.when(jnp.logical_or(chunk < EDGE, edge))(functools.partial(arrive_chunk, chunk))

    def arrive_chunk(chunk):
        for dx, fc in ((0, 0),) + ORDER:
            sx, sq = lax.rem(x + 4 - dx, 4), device(dx, fc)[1]
            got = in_target(chunk, 2 + sx, core, block(sq))
            pltpu.make_async_copy(got, got, in_recv.at[chunk, sx * 4 + sq]).wait()

            @pl.when(jnp.logical_and(has_next, sx >= 2))
            def _():
                z_copy(chunk, sx - 2, sq).start()

    def arrive_z(step):
        for chunk in step_chunks(step):
            @pl.when(jnp.logical_or(chunk < EDGE, edge))
            def _():
                for frame in range(2):
                    for sq in range(4):
                        z_copy(chunk, frame, sq).wait_recv()

    lane = lax.broadcasted_iota(jnp.int32, (CH, COLS), 1)
    first_lane, last_lane = lane == 0, lane == COLS - 1

    def conv(slot, pair):
        rows = []
        for k in range(4):
            row = taken[slot, 2 * pair + k]
            zero = jnp.zeros_like(row)
            rows.append((
                jnp.where(first_lane, zero, pltpu.roll(row, 1, 1)), row,
                jnp.where(last_lane, zero, pltpu.roll(row, COLS - 1, 1)),
            ))
        taps = [
            jnp.concatenate([rows[dy][dx], rows[dy + 1][dx]], axis=1) for dy in range(3) for dx in range(3)
        ]
        lhs = jnp.concatenate([space[tap] for tap in range(9)], axis=1)
        v = jnp.dot(lhs, jnp.concatenate(taps, axis=0), preferred_element_type=jnp.float32) + bias[:, 0:1]
        half = 0.5 * v
        h = (half + half * jnp.tanh(half)).astype(jnp.bfloat16)
        hidden[slot, 2 * pair] = h[:, :COLS]
        hidden[slot, 2 * pair + 1] = h[:, COLS:]

    def temporal(frame, pair):
        lags = [
            jnp.concatenate([hidden[frame + 2 - lag, 2 * pair], hidden[frame + 2 - lag, 2 * pair + 1]], axis=1)
            for lag in range(3)
        ]
        lhs = jnp.concatenate([time[lag] for lag in range(3)], axis=1)
        v = jnp.dot(lhs, jnp.concatenate(lags, axis=0), preferred_element_type=jnp.float32) + bias[:, SHARD:SHARD + 1]
        y = v.astype(jnp.bfloat16).astype(jnp.float32)
        for k in range(2):
            own = taken[frame + 2, 2 * pair + 1 + k].astype(jnp.float32)
            made[frame, 2 * pair + k] = (own + y[:, k * COLS:(k + 1) * COLS]).astype(jnp.bfloat16)

    first_row = start + 6 * core

    def home_copy(frame, tq, pair, step, n):
        src = made.at[frame, pl.ds(2 * pair, n), pl.ds(pl.multiple_of(tq * SHARD, SHARD), SHARD)]
        dst = back.at[pl.ds(first_row + 2 * pair, n)]
        return src, dst, pltpu.make_async_remote_copy(
            src_ref=src, dst_ref=dst, send_sem=out_send.at[step, frame, tq], recv_sem=out_recv,
            device_id={"sp": base + frame, "ch": tq}, device_id_type=MESH,
        )

    def each_home(frame, pair, step, act_far, act_self):
        lacks = jnp.logical_and(jnp.logical_and(core == 1, short), pair == 2)
        for tq in range(4):
            is_me = jnp.logical_and(frame == x, tq == q)
            for n, fits in ((2, jnp.logical_not(lacks)), (1, lacks)):
                src, dst, far = home_copy(frame, tq, pair, step, n)
                pl.when(jnp.logical_and(fits, jnp.logical_not(is_me)))(functools.partial(act_far, far))
                pl.when(jnp.logical_and(fits, is_me))(functools.partial(act_self, src, dst))

    def go_home(frame, pair, step):
        each_home(
            frame, pair, step, lambda far: far.start(),
            lambda src, dst: pltpu.make_async_copy(src, dst, out_recv).start(),
        )

    def swap(lo, n, k):
        return pltpu.make_async_remote_copy(
            src_ref=taken.at[pl.ds(lo, n), 6 - 5 * core], dst_ref=taken.at[pl.ds(lo, n), 7 * core],
            send_sem=swap_send.at[k], recv_sem=swap_recv.at[k], device_id=partner, device_id_type=MESH,
        )

    @pl.when(relays)
    def _():
        weight_copy(0, q, across, 0).wait_recv()
        weight_copy(0, theirs, ring_start, 12).start()

    arrive(0)
    swap(2, 4, 0).start()
    pl.when(jnp.logical_not(relays))(weight_copy(0, q, across, 0).wait_recv)
    for j in range(4):
        if j > 0:
            weight_copy(j, q, across, j).wait_recv()
        weight_copy(j, theirs, partner, 8 + j).start()
    for j in range(4):
        weight_copy(j, q, partner, 4 + j).wait_recv()
        weight_copy(j, theirs, partner, 8 + j).wait_recv()
        keeps[j].wait()
    swap(2, 4, 0).wait_recv()

    def pair_of(step):
        return 2 * (1 - core) + step * (2 * core - 1)

    @pl.loop(0, 3)
    def _(step):
        pair = pair_of(step)

        for slot in range(2, 6):
            conv(slot, pair)
        for frame in (2, 3):
            temporal(frame, pair)
        @pl.when(step < 2)
        def _():
            for frame in (2, 3):
                go_home(frame, pair, step)

        for later in (1, 2):
            pl.when(step == later - 1)(functools.partial(arrive, later))

        @pl.when(has_prev)
        def _():
            for now in range(3):
                @pl.when(step == now)
                def _():
                    arrive_z(now)
                    if now == 0:
                        swap(0, 2, 1).start()
                        swap(0, 2, 1).wait_recv()

            for slot in range(2):
                conv(slot, pair)

        @pl.when(jnp.logical_not(has_prev))
        def _():
            zero = jnp.zeros((CH, COLS), jnp.bfloat16)
            for slot in range(2):
                for k in range(2):
                    hidden[slot, 2 * pair + k] = zero

        for frame in range(2):
            temporal(frame, pair)
        @pl.when(step < 2)
        def _():
            for frame in range(2):
                go_home(frame, pair, step)

        @pl.when(step == 2)
        def _():
            for ahead in (2, 1, 3, 0):
                go_home(lax.rem(x + ahead, 4), pair, step)

    pl.when(jnp.logical_not(skips))(weight_copy(0, q, across, 0).wait_send)
    pl.when(relays)(weight_copy(0, theirs, ring_start, 12).wait_send)
    for j in range(4):
        if j > 0:
            weight_copy(j, q, across, j).wait_send()
        weight_copy(j, q, partner, 4 + j).wait_send()
        weight_copy(j, theirs, partner, 8 + j).wait_send()
    for sends, copy in in_copies:
        pl.when(sends)(copy.wait_send)

    @pl.when(has_next)
    def _():
        for chunk in range(len(CHUNKS)):
            for frame in range(2):
                for sq in range(4):
                    pl.when(jnp.logical_or(chunk < EDGE, edge))(z_copy(chunk, frame, sq).wait_send)

    swap(2, 4, 0).wait_send()

    @pl.when(has_prev)
    def _():
        swap(0, 2, 1).wait_send()

    @pl.loop(0, 3)
    def _(step):
        for frame in range(4):
            each_home(
                frame, pair_of(step), step, lambda far: far.wait_send(), lambda src, dst: None
            )

    pltpu.make_async_copy(back, back, out_recv).wait()


def on_device(latents, space_weight, space_bias, time_weight, time_bias):
    rows_first = latents[:, 0].transpose(1, 0, 2)
    vmem, dma = pltpu.VMEM, pltpu.SemaphoreType.DMA
    bf16, f32 = jnp.bfloat16, jnp.float32
    decoded = pl.pallas_call(
        kernel,
        out_shape=pltpu.VMEM(rows_first.shape, bf16),
        in_specs=[pl.BlockSpec(memory_space=pl.ANY)] * 5,
        out_specs=pl.BlockSpec(memory_space=pl.ANY),
        scratch_shapes=[
            vmem((6, 8, CH, COLS), bf16),
            vmem((6, 6, CH, COLS), bf16),
            vmem((4, 6, CH, COLS), bf16),
            vmem((9, CH, CH), bf16),
            vmem((3, CH, CH), bf16),
            vmem((CH, COLS), f32),
            vmem((SHARD, COLS), f32),
            vmem((2, 1, SHARD), f32),
            dma((6,)),
            dma((len(CHUNKS), 15)),
            dma((len(CHUNKS), 16)),
            dma((len(CHUNKS), 8)),
            dma((len(CHUNKS), 8)),
            dma((2,)),
            dma((2,)),
            dma((13,)),
            dma((12,)),
            dma((3, 4, 4)),
            dma,
        ],
        compiler_params=pltpu.CompilerParams(collective_id=0, has_side_effects=True, vmem_limit_bytes=62 << 20),
        cost_estimate=pl.CostEstimate(flops=6_000_000_000, bytes_accessed=6_000_000, transcendentals=1_200_000),
    )(rows_first, space_weight.transpose(1, 0, 2), time_weight, space_bias[None], time_bias[None])
    return decoded.transpose(1, 0, 2)[:, None]


def solution(mesh):
    return jax.shard_map(
        on_device,
        mesh=mesh,
        in_specs=(
            P("ch", "sp", None, None),
            P("ch", None, None),
            P("ch"),
            P(None, "ch", None),
            P("ch"),
        ),
        out_specs=P("ch", "sp", None, None),
        check_vma=False,
    )
```
